512 devices in a mesh: section: 32 (over z, x), tensor: 16 (over y, core).
Axes of the slice: x: 4, y: 8, z: 8, core: 2. Of those that a mesh axis runs over, the one named last changes fastest.
Arguments:
- travelling_activation: bfloat16 [32, 64, 6144], P('section', None, 'tensor'), may hold values from -45 to 45
- entering: bfloat16 [1, 64, 6144], P(None, None, 'tensor'), may hold values from -45 to 45
- stashed: bfloat16 [32, 2, 64, 6144], P('section', None, None, 'tensor'), may hold values from -45 to 45
- travelling_gradient: bfloat16 [32, 64, 6144], P('section', None, 'tensor'), may hold values from -45 to 45
- returning: bfloat16 [1, 64, 6144], P(None, None, 'tensor'), may hold values from -45 to 45
- frozen: bfloat16 [32, 6144, 6144], P('section', None, 'tensor'), may hold values from -4 to 4
- input_projection: bfloat16 [32, 16, 6144], P('section', None, 'tensor'), may hold values from -0.3125 to 0.3125
- output_projection: bfloat16 [32, 16, 6144], P('section', None, 'tensor'), may hold values from -0.3125 to 0.3125
- magnitude: float32 [32, 6144], P('section', 'tensor'), may hold values from 0.5 to 2
- input_norm_gain: bfloat16 [32, 6144], P('section', 'tensor'), may hold values from 0.5 to 1.5
Outputs:
- act_out: bfloat16 [32, 64, 6144], P('section', None, 'tensor')
- grad_out: bfloat16 [32, 64, 6144], P('section', None, 'tensor')
- grad_mag: float32 [32, 6144], P('section', 'tensor')
- grad_in: float32 [32, 16, 6144], P('section', None, 'tensor')
- grad_outproj: float32 [32, 16, 6144], P('section', None, 'tensor')
- gain_grad: float32 [32, 6144], P('section', 'tensor')
The draws below stay inside these ranges and needn't reach their ends.
All inputs are finite; a program needn't handle non-finite values.
Results may differ from the reference program's by a relative error of at most 0.034.
Values may be sent and summed in bfloat16 or wider, within the bound.
A program may use at most 128 MiB of HBM per device.

```python
import math
import jax
import jax.numpy as jnp
from jax import lax

D = 6144
R = 16
TOK = 64
SLOTS = 2
LAYERS = 32
BLOCKS = 16
COLS = 384


def rough_field(key, layout, offset, spread):
    key_normal = jax.random.fold_in(key, 0)
    key_column = jax.random.fold_in(key, 2)
    key_rows = jax.random.fold_in(key, 3)
    gauss = jnp.clip(jax.random.normal(key_normal, layout, jnp.float32), -4.0, 4.0)
    base = gauss + offset
    column = jnp.arange(D, dtype=jnp.float32) / D
    ramp = jnp.exp(jnp.log(3.0) * (column - 0.5))
    rough = jnp.exp(jax.random.uniform(key_column, (D,), jnp.float32, -0.5, 0.5))
    row_scale = jnp.exp(jax.random.uniform(key_rows, layout[:-1] + (1,), jnp.float32, -spread, spread))
    return (base * ramp * rough * row_scale).astype(jnp.bfloat16)


def draw_travelling_activation(key, part):
    key = jax.random.fold_in(key, 11)
    return rough_field(key, (LAYERS, TOK, D), 0.0, 1.15)


def draw_entering(key, part):
    key = jax.random.fold_in(key, 12)
    return rough_field(key, (SLOTS - 1, TOK, D), 0.0, 1.15)


def draw_stashed(key, part):
    key = jax.random.fold_in(key, 13)
    return rough_field(key, (LAYERS, SLOTS, TOK, D), 0.0, 1.15)


def draw_travelling_gradient(key, part):
    key = jax.random.fold_in(key, 14)
    return rough_field(key, (LAYERS, TOK, D), 0.6, 1.15)


def draw_returning(key, part):
    key = jax.random.fold_in(key, 15)
    return rough_field(key, (SLOTS - 1, TOK, D), 0.6, 1.15)


def draw_frozen(key, part):
    key = jax.random.fold_in(key, 17)
    key_values, key_rows, key_columns = jax.random.split(key, 3)
    column_scale = jnp.exp(jax.random.uniform(key_columns, (1, 1, D), jnp.float32, -0.7, 0.7))
    values = jnp.clip(jax.random.normal(key_values, (LAYERS, D, D), jnp.float32), -4.0, 4.0)
    row_scale = jnp.exp(jax.random.uniform(key_rows, (LAYERS, D, 1), jnp.float32, -1.2, 1.19))
    return (values * row_scale * column_scale / jnp.sqrt(jnp.float32(D))).astype(jnp.bfloat16)


def level_of(key, shape, cuts, smallest, top_value):
    def one(position, parts):
        heights = jax.random.uniform(jax.random.fold_in(jax.random.fold_in(key, 6), position), (parts,), jnp.float32, smallest / len(cuts), top_value / len(cuts))
        return jnp.repeat(jnp.exp(heights), shape[position] // parts).reshape((-1,) + (1,) * (len(shape) - position - 1))

    level = one(*cuts[0])
    for cut in cuts[1:]:
        level = level * one(*cut)
    return level


def normal_values(own_key, shape, scale, reach, cuts=(), held_as=jnp.bfloat16):
    entries = jax.random.normal(own_key, shape, jnp.float32) * scale
    if len(cuts) > 0:
        entries = level_of(own_key, shape, cuts, -0.22, 0.18) * entries
    return jnp.clip(entries, min=-reach, max=reach).astype(held_as)


def setup_inputs(seed: int = 0) -> dict:
    arg_keys = jax.random.split(jax.random.key(seed), 11)
    return {
        "travelling_activation": draw_travelling_activation(jax.random.fold_in(arg_keys[10], 71), 0),
        "entering": draw_entering(jax.random.fold_in(arg_keys[10], 71), 0),
        "stashed": draw_stashed(jax.random.fold_in(arg_keys[10], 71), 0),
        "travelling_gradient": draw_travelling_gradient(jax.random.fold_in(arg_keys[10], 71), 0),
        "returning": draw_returning(jax.random.fold_in(arg_keys[10], 71), 0),
        "frozen": draw_frozen(jax.random.fold_in(arg_keys[10], 71), 0),
        "input_projection": normal_values(arg_keys[6], (LAYERS, R, D), ((R * D) ** -0.25), 0.3125, ((0, 32), (2, 16))),
        "output_projection": normal_values(arg_keys[7], (LAYERS, R, D), ((R * D) ** -0.25), 0.3125, ((0, 32), (2, 16))),
        "magnitude": jnp.clip(jnp.exp(math.log(2.0) - 1.3862944 * jax.random.uniform(arg_keys[8], (LAYERS, D), jnp.float32) ** level_of(arg_keys[8], (LAYERS, D), ((0, 32), (1, 16)), -0.2, 0.2)), 0.5, 2.0),
        "input_norm_gain": jnp.clip(0.5 + 1.0 * jax.random.uniform(arg_keys[9], (LAYERS, D), jnp.float32) ** level_of(arg_keys[9], (LAYERS, D), ((0, 32), (1, 16)), -0.2, 0.2), 0.5, 1.5).astype(jnp.bfloat16),
    }


def build_weight(frozen_layer, adapter_in, adapter_out):
    direction = frozen_layer.astype(jnp.float32) + jnp.dot(adapter_in.T, adapter_out, preferred_element_type=jnp.float32)
    colnorm = jnp.sqrt(lax.optimization_barrier(jnp.sum(direction * direction, axis=0)) + 1e-06)
    return (direction, colnorm)

def normalize_rows(inputs, gain_layer):
    inputs32 = inputs.astype(jnp.float32)
    rscale = lax.rsqrt(lax.optimization_barrier(jnp.sum(inputs32 * inputs32, axis=-1, keepdims=True)) / D + 1e-05)
    normed = (inputs32 * rscale * gain_layer.astype(jnp.float32)).astype(jnp.bfloat16)
    return (inputs32, rscale, normed)

def layer_slot(packed):
    frozen_layer, adapter_in, adapter_out, magnitude_layer, gain_layer, forward_entry, stashed_in, incoming_cotangent = packed
    direction, colnorm = build_weight(frozen_layer, adapter_in, adapter_out)
    merged = (direction * (magnitude_layer / colnorm)).astype(jnp.bfloat16)
    inputs32, rscale, normed = normalize_rows(forward_entry, gain_layer)
    preact = jnp.dot(normed, merged, preferred_element_type=jnp.float32)
    emitted_rows = (inputs32 + jax.nn.silu(preact)).astype(jnp.bfloat16)
    inputs32, rscale, normed = normalize_rows(stashed_in, gain_layer)
    preact = jnp.dot(normed, merged, preferred_element_type=jnp.float32)
    sigmoid_pre = jax.nn.sigmoid(preact)
    silu_slope = sigmoid_pre * (1.0 + preact * (1.0 - sigmoid_pre))
    pre_grad = (incoming_cotangent.astype(jnp.float32) * silu_slope).astype(jnp.bfloat16)
    block_sums = jnp.einsum('tkc,dkc->ktd', pre_grad.astype(jnp.float32).reshape(TOK, BLOCKS, COLS), merged.astype(jnp.float32).reshape(D, BLOCKS, COLS))
    rounded = lax.optimization_barrier(block_sums.astype(jnp.bfloat16)).astype(jnp.float32)
    norm_grad = lax.optimization_barrier(jnp.sum(rounded, axis=0))
    rowdot = lax.optimization_barrier(jnp.sum(normed.astype(jnp.float32) * norm_grad, axis=-1, keepdims=True))
    gain32 = gain_layer.astype(jnp.float32)
    returned_gradient = (incoming_cotangent.astype(jnp.float32) + rscale * gain32 * norm_grad - inputs32 * rscale * rscale * rowdot / D).astype(jnp.bfloat16)
    gain_term = lax.optimization_barrier(jnp.sum(norm_grad * inputs32 * rscale, axis=0))
    return (emitted_rows, returned_gradient, normed, pre_grad, gain_term)

def weight_pass(packed):
    frozen_layer, adapter_in, adapter_out, magnitude_layer, normed_rows, pregrad_rows = packed
    direction, colnorm = build_weight(frozen_layer, adapter_in, adapter_out)
    grad_w = jnp.dot(normed_rows.T, pregrad_rows, preferred_element_type=jnp.float32) / (SLOTS * TOK)
    col_inner = lax.optimization_barrier(jnp.sum(grad_w * direction, axis=0))
    grad_mag = col_inner / colnorm
    dir_grad = (magnitude_layer / colnorm * (grad_w - direction * (col_inner / (colnorm * colnorm)))).astype(jnp.bfloat16)
    grad_outproj = jnp.dot(adapter_in, dir_grad, preferred_element_type=jnp.float32)
    grad_in = jnp.dot(adapter_out, dir_grad.T, preferred_element_type=jnp.float32)
    return (grad_mag, grad_in, grad_outproj)

def reference(travelling_activation, entering, stashed, travelling_gradient, returning, frozen, input_projection, output_projection, magnitude, input_norm_gain):
    forward_entry = travelling_activation
    cotangent_rows = travelling_gradient
    normed_list = []
    pregrad_list = []
    gain_total = jnp.zeros((LAYERS, D), jnp.float32)
    emitted_rows = travelling_activation
    returned_gradient = travelling_gradient
    for slot_index in range(SLOTS):
        if slot_index > 0:
            forward_entry = jnp.concatenate([entering[slot_index - 1][None], emitted_rows[:-1]], axis=0)
            cotangent_rows = jnp.concatenate([returned_gradient[1:], returning[slot_index - 1][None]], axis=0)
        emitted_rows, returned_gradient, normed, pre_grad, gain_term = lax.map(layer_slot, (frozen, input_projection, output_projection, magnitude, input_norm_gain, forward_entry, stashed[:, slot_index], cotangent_rows))
        normed_list.append(normed)
        pregrad_list.append(pre_grad)
        gain_total = gain_total + gain_term
    normed_stack = jnp.concatenate(normed_list, axis=1)
    pregrad_stack = jnp.concatenate(pregrad_list, axis=1)
    grad_mag, grad_in, grad_outproj = lax.map(weight_pass, (frozen, input_projection, output_projection, magnitude, normed_stack, pregrad_stack))
    gain_grad = gain_total / (SLOTS * TOK)
    return (emitted_rows, returned_gradient, grad_mag, grad_in, grad_outproj, gain_grad)
```

```python
import jax
import jax.numpy as jnp
from jax import lax
from jax.experimental import pallas as pl
from jax.experimental.pallas import tpu as pltpu
from jax.sharding import PartitionSpec as P

F32 = jnp.float32
BF16 = jnp.bfloat16
CHIPS = 8
TOK = 64
RANK = 16
COLS = 384
PAIR = 2 * COLS
FEATURES = CHIPS * PAIR
SLOTS = 2
ORDER = (3, 5, 4, 1, 7, 2, 6, 0)
COPIES = 160


def dot(a, b):
    return jnp.dot(a, b, preferred_element_type=F32)


def dot_nt(a, b):
    return lax.dot_general(a, b, (((1,), (1,)), ((), ())), preferred_element_type=F32)


def dot_tn(a, b):
    return lax.dot_general(a, b, (((0,), (0,)), ((), ())), preferred_element_type=F32)


def lane_groups(x):
    total = x[:, 0:128]
    for start in range(128, x.shape[1], 128):
        total = total + x[:, start : start + 128]
    return total


def row_to_column(row):
    square = jnp.transpose(jnp.broadcast_to(row, (128, 128)))
    return square[0:TOK, 0:1]


def column_partials_to_row(partials):
    padded = jnp.concatenate([partials, jnp.zeros((128 - TOK, 128), F32)], axis=0)
    return jnp.sum(jnp.transpose(padded), axis=0, keepdims=True)


def kernel(
    act_hbm, ent_hbm, sta_hbm, tg_hbm, ret_hbm, frozen_hbm, ain_hbm, aout_hbm, mag_ref, gain_ref,
    act_o, grad_o, mag_o, gin_o, gout_o, gain_o,
    fz, w, g0, g1, g2, g3, gn, zn0, zn1, tg, ent, ret, aout, em, x1, gr, gx,
    pb0, sb0, sv0, rv0, pb1, sb1, sv1, rv1, rd0, rd1, ssem, rsem, lsem,
):
    me = lax.axis_index("tensor")
    sec = lax.axis_index("section")
    sections = lax.axis_size("section")
    y = me // 2
    core = me - 2 * y
    mine = pl.ds(pl.multiple_of(core * COLS, 128), COLS)
    other = pl.ds(pl.multiple_of((1 - core) * COLS, 128), COLS)

    def chip(offset):
        return {"tensor": lax.rem(y + offset + CHIPS, CHIPS) * 2 + core}

    sibling = {"tensor": me + 1 - 2 * core}
    after = {"section": lax.rem(sec + 1, sections)}
    before = {"section": lax.rem(sec + sections - 1, sections)}

    counter = [0]
    started = []

    def send(src, dst, device):
        index = counter[0]
        counter[0] += 1
        copy = pltpu.make_async_remote_copy(
            src_ref=src, dst_ref=dst, send_sem=ssem.at[index], recv_sem=rsem.at[index],
            device_id=device, device_id_type=MESH,
        )
        copy.start()
        started.append(copy)
        return copy

    locals_ = []

    def load(src, dst):
        copy = pltpu.make_async_copy(src, dst, lsem.at[len(locals_)])
        copy.start()
        locals_.append(copy)
        return copy

    l_s0 = load(sta_hbm.at[0, 0], g0.at[0, 0:TOK, mine])
    l_a = load(ain_hbm.at[0], g0.at[0, TOK : TOK + RANK, mine])
    l_fz = load(frozen_hbm.at[0], fz)
    l_p = load(aout_hbm.at[0], aout)
    l_t0 = load(act_hbm.at[0], g1.at[0, :, mine])
    l_tg = load(tg_hbm.at[0], tg)
    l_s1 = load(sta_hbm.at[0, 1], g2.at[0, :, mine])
    l_ent = load(ent_hbm.at[0], ent)
    l_ret = load(ret_hbm.at[0], ret)

    barrier = pltpu.get_barrier_semaphore()
    peers = [chip(1), chip(-1), chip(2), chip(-2), sibling, after, before]
    for peer in peers:
        pl.semaphore_signal(barrier, inc=1, device_id=peer, device_id_type=MESH)
    gain = gain_ref[...].astype(F32)
    gn[0, 0:1, mine] = gain
    pl.semaphore_wait(barrier, len(peers))

    class Gather:
        def __init__(self, ref, rows, split, lead=None):
            self.parts = [(ref, slice(0, rows), split)]
            if lead is not None:
                self.parts = [(lead, slice(0, 1), None)] + self.parts
            self.near = {}
            self.far = {}
            self.sib = {}

        def begin(self):
            for offset in (2, -2, 1, -1):
                slot = (-offset) % CHIPS
                for n, (ref, rows, _) in enumerate(self.parts):
                    self.near[slot, n] = send(ref.at[0, rows, mine], ref.at[slot, rows, mine], chip(offset))
                if offset == 2:
                    self.share(0)

        def share(self, slot):
            for n, (ref, rows, _) in enumerate(self.parts):
                self.sib[slot, n] = send(ref.at[slot, rows, mine], ref.at[slot, rows, mine], sibling)

        def pass_on(self):
            for held, step, low in ((6, 1, True), (2, -1, False)):
                for n, (ref, rows, split) in enumerate(self.parts):
                    self.near[held, n].wait_recv()
                    slot = (held - step) % CHIPS
                    self.far[slot, n] = [send(ref.at[held, rows, mine], ref.at[slot, rows, mine], chip(step))]
                    if split is None:
                        if low:
                            self.far[4, n] = [send(ref.at[held, rows, mine], ref.at[4, rows, mine], chip(2))]
                    else:
                        part = slice(0, split) if low else slice(split, rows.stop)
                        self.far.setdefault((4, n), []).append(
                            send(ref.at[held, part, mine], ref.at[4, part, mine], chip(2 * step))
                        )
                self.share(held)

        def share_near(self):
            for slot in (7, 1):
                for n in range(len(self.parts)):
                    self.near[slot, n].wait_recv()
                self.share(slot)

        def share_far(self):
            for slot in (5, 3, 4):
                for n in range(len(self.parts)):
                    for copy in self.far[slot, n]:
                        copy.wait_recv()
                self.share(slot)

        def ready(self, slot):
            for n in range(len(self.parts)):
                self.sib[slot, n].wait_recv()

    def base_of(slot):
        return pl.multiple_of(lax.rem(y + slot, CHIPS) * PAIR, PAIR)

    def build(slot, norms):
        base = base_of(slot)
        for part in range(3):
            lanes = slice(part * 256, (part + 1) * 256)
            rows = pl.ds(pl.multiple_of(base + part * 256, 256), 256)
            direction = fz[rows, :].astype(F32) + dot_tn(g0[slot, TOK : TOK + RANK, lanes], aout[...])
            w[rows, :] = direction.astype(BF16)
            norms = norms + jnp.sum((direction * direction).reshape(32, 8, COLS), axis=0)
        return norms

    def chunk(ref, slot, squares, total, with_adapter=False):
        z = ref[slot, 0:TOK, :].astype(F32)
        squares = squares + lane_groups(z * z)
        scaled = (z * gn[slot, 0:1, :]).astype(BF16)
        if with_adapter:
            scaled = jnp.concatenate([scaled, ref[slot, TOK : TOK + RANK, :]], axis=0)
        total = total + dot(scaled, w[pl.ds(base_of(slot), PAIR), :])
        return squares, total

    def rscale_of(squares):
        return lax.rsqrt(jnp.sum(squares, axis=1, keepdims=True) / FEATURES + 1e-05)

    def normalise(ref, out, rscale):
        for slot in range(CHIPS):
            z = ref[slot, 0:TOK, :].astype(F32)
            out[slot] = (z * rscale * gn[slot, 0:1, :]).astype(BF16)

    def slope_of(preact):
        sig = 1.0 / (1.0 + jnp.exp(-preact))
        return sig * (1.0 + preact * (1.0 - sig))

    class Scatter:
        def __init__(self, rows, split, pb, sb, sv, rv, rd):
            self.rows, self.split = rows, split
            self.pb, self.sb, self.sv, self.rv, self.rd = pb, sb, sv, rv, rd

        def compute(self, lhs, dots, extra=None):
            self.rd[0] = jnp.broadcast_to(dots, (8, 128))
            self.rd_sib = send(self.rd.at[0], self.rd.at[1], sibling)
            for n, slot in enumerate(ORDER):
                value = dot_nt(lhs, w[pl.ds(base_of(slot), PAIR), :])
                if extra is not None:
                    value = jnp.concatenate([value[0:TOK], value[TOK:] + extra(slot)], axis=0)
                self.pb[n] = value.astype(BF16)
                if n == 2:
                    self.first = send(self.pb.at[0:3, :, other], self.sb.at[0:3], sibling)
            self.second = send(self.pb.at[3:8, :, other], self.sb.at[3:8], sibling)

        def pair_sum(self, n):
            return self.pb[n, :, mine].astype(F32) + self.sb[n].astype(F32)

        def stage_one(self):
            rd, rv, sv = self.rd, self.rv, self.sv
            self.first.wait_recv()
            sv[2] = self.pair_sum(2).astype(BF16)
            low, high = slice(0, self.split), slice(self.split, self.rows)
            self.r4a = send(sv.at[2, low], rv.at[2, low], chip(-2))
            self.r4b = send(sv.at[2, high], rv.at[2, high], chip(2))
            sv[0] = self.pair_sum(0).astype(BF16)
            self.r1 = send(sv.at[0], rv.at[0], chip(1))
            sv[1] = self.pair_sum(1).astype(BF16)
            self.r2 = send(sv.at[1], rv.at[1], chip(-1))
            self.rd_sib.wait_recv()
            rd[2] = rd[0] + rd[1]
            self.rd_a = send(rd.at[2], rd.at[3], chip(1))
            self.rd_b = send(rd.at[2], rd.at[4], chip(-1))
            self.rd_c = send(rd.at[2], rd.at[5], chip(-2))

        def stage_one_direct(self):
            rv, sv = self.rv, self.sv
            self.second.wait_recv()
            sv[3] = self.pair_sum(3).astype(BF16)
            self.d1 = send(sv.at[3], rv.at[3], chip(1))
            sv[4] = self.pair_sum(4).astype(BF16)
            self.d2 = send(sv.at[4], rv.at[4], chip(-1))

        def stage_two(self):
            rv, sv, rd = self.rv, self.sv, self.rd
            split = self.split
            self.r1.wait_recv()
            self.r4b.wait_recv()
            total = self.pair_sum(5) + rv[0].astype(F32)
            total = jnp.concatenate([total[0:split], total[split:] + rv[2, split:].astype(F32)], axis=0)
            sv[5] = total.astype(BF16)
            self.e1 = send(sv.at[5], rv.at[5], chip(2))
            self.r2.wait_recv()
            self.r4a.wait_recv()
            total = self.pair_sum(6) + rv[1].astype(F32)
            total = jnp.concatenate([total[0:split] + rv[2, 0:split].astype(F32), total[split:]], axis=0)
            sv[6] = total.astype(BF16)
            self.e2 = send(sv.at[6], rv.at[6], chip(-2))
            self.rd_a.wait_recv()
            self.rd_b.wait_recv()
            self.rd_c.wait_recv()
            rd[6] = rd[2] + rd[3]
            self.rd_e = send(rd.at[6], rd.at[8], chip(2))
            rd[7] = rd[2] + rd[4] + rd[5]
            self.rd_f = send(rd.at[7], rd.at[9], chip(-2))

        def final(self):
            rv, rd = self.rv, self.rd
            total = self.pair_sum(7)
            self.d1.wait_recv()
            self.d2.wait_recv()
            total = total + rv[3].astype(F32) + rv[4].astype(F32)
            self.rd_e.wait_recv()
            self.rd_f.wait_recv()
            dots = rd[2] + rd[3] + rd[4] + rd[8] + rd[9]
            self.e1.wait_recv()
            self.e2.wait_recv()
            total = total + rv[5].astype(F32) + rv[6].astype(F32)
            return total, row_to_column(dots[0:1, :])

    ga_s0 = Gather(g0, TOK + RANK, 48, lead=gn)
    ga_t0 = Gather(g1, TOK, 32)
    ga_s1 = Gather(g2, TOK, 32)
    ga_t1 = Gather(g3, TOK, 32)
    rs0 = Scatter(TOK, 32, pb0, sb0, sv0, rv0, rd0)
    rs1 = Scatter(TOK + RANK, 48, pb1, sb1, sv1, rv1, rd1)

    def fresh():
        return jnp.zeros((TOK, 128), F32), jnp.zeros((TOK, COLS), F32)

    l_s0.wait()
    l_a.wait()
    ga_s0.begin()
    l_fz.wait()
    l_p.wait()
    norms = jnp.zeros((8, COLS), F32)
    squares = jnp.zeros((TOK, 128), F32)
    total = jnp.zeros((TOK + RANK, COLS), F32)
    ga_s0.ready(0)
    norms = build(0, norms)
    squares, total = chunk(g0, 0, squares, total, True)
    ga_s0.pass_on()
    l_t0.wait()
    ga_t0.begin()
    ga_s0.share_near()
    for slot in (6, 2, 7, 1):
        ga_s0.ready(slot)
        norms = build(slot, norms)
        squares, total = chunk(g0, slot, squares, total, True)
    ga_s0.share_far()
    for slot in (5, 3, 4):
        ga_s0.ready(slot)
        norms = build(slot, norms)
        squares, total = chunk(g0, slot, squares, total, True)
    norm_squares = jnp.sum(norms, axis=0, keepdims=True) + 1e-06
    colnorm = jnp.sqrt(norm_squares)
    col_scale = mag_ref[...] / colnorm
    r0 = rscale_of(squares)
    raw0 = total[0:TOK] * r0
    adapter_direction = total[TOK:]
    preact = raw0 * col_scale
    l_tg.wait()
    cot0 = tg[...].astype(F32)
    pg = cot0 * slope_of(preact)
    pgs0 = (pg * col_scale).astype(BF16)
    inner = jnp.sum(pg * raw0, axis=0, keepdims=True)
    rs0.compute(pgs0, column_partials_to_row(lane_groups(pg * preact)))
    ga_t0.pass_on()
    l_s1.wait()
    rs0.stage_one()
    ga_s1.begin()
    rs0.stage_one_direct()
    ga_t0.share_near()
    squares, total = fresh()
    for slot in (0, 6, 2, 7, 1):
        ga_t0.ready(slot)
        squares, total = chunk(g1, slot, squares, total)
    rs0.stage_two()
    ga_t0.share_far()
    for slot in (5, 3, 4):
        ga_t0.ready(slot)
        squares, total = chunk(g1, slot, squares, total)
    preact = total * rscale_of(squares) * col_scale
    emitted = g1[0, :, mine].astype(F32) + preact / (1.0 + jnp.exp(-preact))
    l_ent.wait()
    em[...] = jnp.where(sec == sections - 1, ent[...], emitted.astype(BF16))
    shift_act = send(em, g3.at[0, :, mine], after)
    ga_s1.pass_on()
    normalise(g0, zn0, r0)
    norm_grad, rowdot = rs0.final()
    own = g0[0, 0:TOK, mine].astype(F32)
    returned = cot0 + r0 * gain * norm_grad - own * (r0 * r0 * rowdot / FEATURES)
    l_ret.wait()
    gr[...] = jnp.where(sec == 0, ret[...], returned.astype(BF16))
    shift_cot = send(gr, gx, before)
    gain_total = jnp.sum(norm_grad * own * r0, axis=0, keepdims=True)
    ga_s1.share_near()
    shift_act.wait_recv()
    ga_t1.begin()
    squares, total = fresh()
    for slot in (0, 6, 2, 7, 1):
        ga_s1.ready(slot)
        squares, total = chunk(g2, slot, squares, total)
    ga_s1.share_far()
    for slot in (5, 3, 4):
        ga_s1.ready(slot)
        squares, total = chunk(g2, slot, squares, total)
    r1 = rscale_of(squares)
    raw1 = total * r1
    preact = raw1 * col_scale
    slope = slope_of(preact)
    normalise(g2, zn1, r1)
    factor = aout[...]
    mean = 1.0 / (SLOTS * TOK)
    weights0 = dot_nt(factor, pgs0)
    shift_cot.wait_recv()
    cot1 = gx[...].astype(F32)
    pg = cot1 * slope
    pgs1 = (pg * col_scale).astype(BF16)
    inner = (inner + jnp.sum(pg * raw1, axis=0, keepdims=True)) * mean
    ratio = inner / norm_squares
    scaled_ratio = col_scale * ratio
    weights = (jnp.concatenate([weights0, dot_nt(factor, pgs1)], axis=1) * mean).astype(BF16)
    shrunk = (factor.astype(F32) * -scaled_ratio).astype(BF16)

    def column_extra(slot):
        return dot(weights, jnp.concatenate([zn0[slot], zn1[slot]], axis=0))

    rs1.compute(
        jnp.concatenate([pgs1, shrunk], axis=0),
        column_partials_to_row(lane_groups(pg * preact)),
        column_extra,
    )
    rs1.stage_one()
    ga_t1.pass_on()
    rs1.stage_one_direct()
    ga_t1.share_near()
    mag_o[...] = inner / colnorm
    product = jnp.zeros((RANK, TOK * SLOTS), F32)
    for slot in range(CHIPS):
        product = product + dot_nt(
            g0[slot, TOK : TOK + RANK, :], jnp.concatenate([zn0[slot], zn1[slot]], axis=0)
        )
    upper = product.astype(BF16)
    lower = (product - upper.astype(F32)).astype(BF16)
    both = dot(jnp.concatenate([upper, lower], axis=0), jnp.concatenate([pgs0, pgs1], axis=0))
    gout_o[0] = (both[0:RANK] + both[RANK:]) * mean - adapter_direction * scaled_ratio
    rs1.stage_two()
    squares, total = fresh()
    for slot in (0, 6, 2, 7, 1):
        ga_t1.ready(slot)
        squares, total = chunk(g3, slot, squares, total)
    ga_t1.share_far()
    for slot in (5, 3, 4):
        ga_t1.ready(slot)
        squares, total = chunk(g3, slot, squares, total)
    preact = total * rscale_of(squares) * col_scale
    act_o[0] = (g3[0, :, mine].astype(F32) + preact / (1.0 + jnp.exp(-preact))).astype(BF16)
    norm_grad, rowdot = rs1.final()
    gin_o[0] = norm_grad[TOK:]
    norm_grad = norm_grad[0:TOK]
    own = g2[0, :, mine].astype(F32)
    grad_o[0] = (cot1 + r1 * gain * norm_grad - own * (r1 * r1 * rowdot / FEATURES)).astype(BF16)
    gain_total = gain_total + jnp.sum(norm_grad * own * r1, axis=0, keepdims=True)
    gain_o[...] = gain_total * mean
    for copy in started:
        copy.wait_send()


MESH = pl.DeviceIdType.MESH


def local(*args):
    anywhere = pl.BlockSpec(memory_space=pl.ANY)
    vmem = pl.BlockSpec(memory_space=pltpu.VMEM)
    rows1 = TOK + RANK

    def scatter_buffers(rows):
        return [
            pltpu.VMEM((8, rows, PAIR), BF16),
            pltpu.VMEM((8, rows, COLS), BF16),
            pltpu.VMEM((7, rows, COLS), BF16),
            pltpu.VMEM((7, rows, COLS), BF16),
        ]

    gathered = pltpu.VMEM((CHIPS, TOK, PAIR), BF16)
    block = pltpu.VMEM((TOK, COLS), BF16)
    return pl.pallas_call(
        kernel,
        out_shape=(
            jax.ShapeDtypeStruct((1, TOK, COLS), BF16),
            jax.ShapeDtypeStruct((1, TOK, COLS), BF16),
            jax.ShapeDtypeStruct((1, COLS), F32),
            jax.ShapeDtypeStruct((1, RANK, COLS), F32),
            jax.ShapeDtypeStruct((1, RANK, COLS), F32),
            jax.ShapeDtypeStruct((1, COLS), F32),
        ),
        in_specs=[anywhere] * 8 + [vmem] * 2,
        out_specs=(vmem,) * 6,
        scratch_shapes=[
            pltpu.VMEM((FEATURES, COLS), BF16),
            pltpu.VMEM((FEATURES, COLS), BF16),
            pltpu.VMEM((CHIPS, rows1, PAIR), BF16),
            gathered,
            gathered,
            gathered,
            pltpu.VMEM((CHIPS, 8, PAIR), F32),
            gathered,
            gathered,
            block,
            block,
            block,
            pltpu.VMEM((RANK, COLS), BF16),
            block,
            block,
            block,
            block,
            *scatter_buffers(TOK),
            *scatter_buffers(rows1),
            pltpu.VMEM((10, 8, 128), F32),
            pltpu.VMEM((10, 8, 128), F32),
            pltpu.SemaphoreType.DMA((COPIES,)),
            pltpu.SemaphoreType.DMA((COPIES,)),
            pltpu.SemaphoreType.DMA((9,)),
        ],
        compiler_params=pltpu.CompilerParams(
            collective_id=0, has_side_effects=True, vmem_limit_bytes=44 * 2**20
        ),
        name="window",
    )(*args)


def solution(mesh):
    in_specs = (
        P("section", None, "tensor"),
        P(None, None, "tensor"),
        P("section", None, None, "tensor"),
        P("section", None, "tensor"),
        P(None, None, "tensor"),
        P("section", None, "tensor"),
        P("section", None, "tensor"),
        P("section", None, "tensor"),
        P("section", "tensor"),
        P("section", "tensor"),
    )
    out_specs = (
        P("section", None, "tensor"),
        P("section", None, "tensor"),
        P("section", "tensor"),
        P("section", None, "tensor"),
        P("section", None, "tensor"),
        P("section", "tensor"),
    )
    return jax.shard_map(local, mesh=mesh, in_specs=in_specs, out_specs=out_specs, check_vma=False)
```

```python
import jax
import jax.numpy as jnp
from jax import lax
from jax.experimental import pallas as pl
from jax.experimental.pallas import tpu as pltpu
from jax.sharding import PartitionSpec as P

F32 = jnp.float32
BF16 = jnp.bfloat16
MESH = pl.DeviceIdType.MESH
CHIPS = 8
TOK = 64
RANK = 16
COLS = 384
PAIR = 2 * COLS
FEATURES = CHIPS * PAIR
SLOTS = 2
ORDER = (3, 5, 4, 1, 7, 2, 6, 0)
COPIES = 160


def dot(a, b):
    return jnp.dot(a, b, preferred_element_type=F32)


def dot_nt(a, b):
    return lax.dot_general(a, b, (((1,), (1,)), ((), ())), preferred_element_type=F32)


def dot_tn(a, b):
    return lax.dot_general(a, b, (((0,), (0,)), ((), ())), preferred_element_type=F32)


def lane_groups(x):
    total = x[:, 0:128]
    for start in range(128, x.shape[1], 128):
        total = total + x[:, start : start + 128]
    return total


def kernel(
    act_hbm, ent_hbm, sta_hbm, tg_hbm, ret_hbm, frozen_hbm, ain_hbm, aout_hbm, mag_ref, gain_ref,
    act_o, grad_o, mag_o, gin_o, gout_o, gain_o,
    fz, w, g0, g1, g2, g3, gn, zn0, zn1, tg, tgx, ent, ret, aout, em, gx,
    pb0, sb0, sv0, rv0, pb1, sb1, sv1, rv1, gt, gts, gtv, gtr, ssem, rsem, lsem,
):
    me = lax.axis_index("tensor")
    sec = lax.axis_index("section")
    sections = lax.axis_size("section")
    y = me // 2
    core = me - 2 * y
    mine = pl.ds(pl.multiple_of(core * COLS, 128), COLS)
    other = pl.ds(pl.multiple_of((1 - core) * COLS, 128), COLS)

    def chip(offset):
        return {"tensor": lax.rem(y + offset + CHIPS, CHIPS) * 2 + core}

    def previous(offset):
        return {"section": sec - 1, **chip(offset)}

    def following(offset):
        return {"section": sec + 1, **chip(offset)}

    sibling = {"tensor": me + 1 - 2 * core}
    has_previous = sec > 0
    has_following = sec < sections - 1
    no_previous = jnp.logical_not(has_previous)

    counter = [0]
    started = []

    def send(src, dst, device, condition=None, arrival=None):
        index = counter[0]
        counter[0] += 1
        arrival = index if arrival is None else arrival
        copy = pltpu.make_async_remote_copy(
            src_ref=src, dst_ref=dst, send_sem=ssem.at[index], recv_sem=rsem.at[arrival],
            device_id=device, device_id_type=MESH,
        )
        if condition is None:
            copy.start()
        else:
            pl.when(condition)(copy.start)
        started.append((copy, condition))
        return copy

    locals_ = []

    def load(src, dst):
        copy = pltpu.make_async_copy(src, dst, lsem.at[len(locals_)])
        copy.start()
        locals_.append(copy)
        return copy

    l_s0 = load(sta_hbm.at[0, 0], g0.at[0, 0:TOK, mine])
    l_a = load(ain_hbm.at[0], g0.at[0, TOK : TOK + RANK, mine])
    l_fz = load(frozen_hbm.at[0], fz)
    l_p = load(aout_hbm.at[0], aout)
    l_t0 = load(act_hbm.at[0], g1.at[0, :, mine])
    l_tg = load(tg_hbm.at[0], tg)
    l_s1 = load(sta_hbm.at[0, 1], g2.at[0, :, mine])
    l_ent = load(ent_hbm.at[0], ent)
    l_ret = load(ret_hbm.at[0], ret)

    barrier = pltpu.get_barrier_semaphore()
    near = (0, 1, -1, 2, -2)

    def greet(peers):
        for peer in peers:
            pl.semaphore_signal(barrier, inc=1, device_id=peer, device_id_type=MESH)

    greet([chip(offset) for offset in near[1:]] + [sibling])

    @pl.when(has_previous)
    def _():
        greet([previous(offset) for offset in near])

    @pl.when(has_following)
    def _():
        greet([following(offset) for offset in near])

    gain = gain_ref[...].astype(F32)
    gn[0, 0:1, mine] = gain
    expected = len(near) * (1 + jnp.where(has_following, 1, 0) + jnp.where(has_previous, 1, 0))
    pl.semaphore_wait(barrier, expected)

    class Gather:
        def __init__(self, ref, rows, split, lead=None):
            self.parts = [(ref, slice(0, rows), split)]
            if lead is not None:
                self.parts = [(lead, slice(0, 1), None)] + self.parts
            self.near = {}
            self.far = {}
            self.sib = {}

        def begin(self):
            for offset in (2, -2, 1, -1):
                slot = (-offset) % CHIPS
                for n, (ref, rows, _) in enumerate(self.parts):
                    self.near[slot, n] = send(ref.at[0, rows, mine], ref.at[slot, rows, mine], chip(offset))
                if offset == 2:
                    self.share(0)

        def begin_next(self, src, first):
            for offset in (2, -2, 0, 1, -1):
                slot = (-offset) % CHIPS
                ref = self.parts[0][0]
                arrival = counter[0]
                copy = send(src, ref.at[slot, :, mine], following(offset), has_following)
                if offset == 0:
                    self.own = copy
                else:
                    self.near[slot, 0] = copy
                    send(first, ref.at[slot, :, mine], chip(offset), no_previous, arrival)

        def share_own(self, first):
            ref = self.parts[0][0]

            @pl.when(has_previous)
            def _():
                self.own.wait_recv()

            @pl.when(no_previous)
            def _():
                ref[0, :, mine] = first[...]

            self.share(0)

        def share(self, slot):
            for n, (ref, rows, _) in enumerate(self.parts):
                self.sib[slot, n] = send(ref.at[slot, rows, mine], ref.at[slot, rows, mine], sibling)

        def pass_on(self):
            for held, step, low in ((6, 1, True), (2, -1, False)):
                for n, (ref, rows, split) in enumerate(self.parts):
                    self.near[held, n].wait_recv()
                    slot = (held - step) % CHIPS
                    self.far[slot, n] = [send(ref.at[held, rows, mine], ref.at[slot, rows, mine], chip(step))]
                    if split is None:
                        if low:
                            self.far[4, n] = [send(ref.at[held, rows, mine], ref.at[4, rows, mine], chip(2))]
                    else:
                        part = slice(0, split) if low else slice(split, rows.stop)
                        self.far.setdefault((4, n), []).append(
                            send(ref.at[held, part, mine], ref.at[4, part, mine], chip(2 * step))
                        )
                self.share(held)

        def share_near(self):
            for slot in (7, 1):
                for n in range(len(self.parts)):
                    self.near[slot, n].wait_recv()
                self.share(slot)

        def share_far(self):
            for slot in (5, 3, 4):
                for n in range(len(self.parts)):
                    for copy in self.far[slot, n]:
                        copy.wait_recv()
                self.share(slot)

        def ready(self, slot):
            for n in range(len(self.parts)):
                self.sib[slot, n].wait_recv()

    def base_of(slot):
        return pl.multiple_of(lax.rem(y + slot, CHIPS) * PAIR, PAIR)

    def build(slot, norms):
        base = base_of(slot)
        for part in range(3):
            lanes = slice(part * 256, (part + 1) * 256)
            rows = pl.ds(pl.multiple_of(base + part * 256, 256), 256)
            direction = fz[rows, :].astype(F32) + dot_tn(g0[slot, TOK : TOK + RANK, lanes], aout[...])
            w[rows, :] = direction.astype(BF16)
            norms = norms + jnp.sum((direction * direction).reshape(32, 8, COLS), axis=0)
        return norms

    def chunk(ref, slot, squares, total, with_adapter=False):
        z = ref[slot, 0:TOK, :].astype(F32)
        squares = squares + lane_groups(z * z)
        scaled = (z * gn[slot, 0:1, :]).astype(BF16)
        if with_adapter:
            scaled = jnp.concatenate([scaled, ref[slot, TOK : TOK + RANK, :]], axis=0)
        total = total + dot(scaled, w[pl.ds(base_of(slot), PAIR), :])
        return squares, total

    def rscale_of(squares):
        return lax.rsqrt(jnp.sum(squares, axis=1, keepdims=True) / FEATURES + 1e-05)

    def normalise(ref, out, rscale):
        for slot in range(CHIPS):
            z = ref[slot, 0:TOK, :].astype(F32)
            out[slot] = (z * rscale * gn[slot, 0:1, :]).astype(BF16)

    def slope_of(preact):
        sig = 1.0 / (1.0 + jnp.exp(-preact))
        return sig * (1.0 + preact * (1.0 - sig))

    class Scatter:
        def __init__(self, rows, split, pb, sb, sv, rv, back):
            self.rows, self.split = rows, split
            self.pb, self.sb, self.sv, self.rv, self.back = pb, sb, sv, rv, back

        def prepare(self, lhs, ref, rscale, dots, extra=None):
            self.args = lhs, ref, rscale, rscale * rscale * dots / FEATURES, extra

        def compute(self, start, stop):
            lhs, ref, rscale, tilt, extra = self.args
            for n in range(start, stop):
                slot = ORDER[n]
                value = dot_nt(lhs, w[pl.ds(base_of(slot), PAIR), :])
                z = ref[slot, 0:TOK, :].astype(F32)
                scaled = value[0:TOK] * rscale
                term = jnp.sum(scaled * z, axis=0, keepdims=True)
                gt[n : n + 1, :] = term if extra is None else gt[n : n + 1, :] + term
                result = scaled * gn[slot, 0:1, :] - z * tilt
                if extra is not None:
                    result = jnp.concatenate([result, value[TOK:] + extra(slot)], axis=0)
                self.pb[n] = result.astype(BF16)
            return send(self.pb.at[start:stop, :, other], self.sb.at[start:stop], sibling)

        def compute_first(self):
            self.first = self.compute(0, 3)

        def compute_second(self):
            self.second = self.compute(3, 8)

        def pair_sum(self, n):
            return self.pb[n, :, mine].astype(F32) + self.sb[n].astype(F32)

        def deliver(self, n, offset):
            src, dst = self.sv.at[n], self.rv.at[n]
            if self.back:
                return send(src, dst, previous(offset), has_previous)
            return send(src, dst, chip(offset))

        def stage_one(self):
            rv, sv = self.rv, self.sv
            self.first.wait_recv()
            sv[2] = self.pair_sum(2).astype(BF16)
            low, high = slice(0, self.split), slice(self.split, self.rows)
            self.r4a = send(sv.at[2, low], rv.at[2, low], chip(-2))
            self.r4b = send(sv.at[2, high], rv.at[2, high], chip(2))
            sv[0] = self.pair_sum(0).astype(BF16)
            self.r1 = send(sv.at[0], rv.at[0], chip(1))
            sv[1] = self.pair_sum(1).astype(BF16)
            self.r2 = send(sv.at[1], rv.at[1], chip(-1))

        def stage_one_direct(self):
            self.second.wait_recv()
            self.last = []
            for n, offset in ((3, 1), (4, -1)):
                self.sv[n] = self.pair_sum(n).astype(BF16)
                self.last.append(self.deliver(n, offset))
            if self.back:
                self.sv[7] = self.pair_sum(7).astype(BF16)
                self.last.append(self.deliver(7, 0))

        def stage_two(self):
            rv, split = self.rv, self.split
            self.r1.wait_recv()
            self.r4b.wait_recv()
            total = self.pair_sum(5) + rv[0].astype(F32)
            total = jnp.concatenate([total[0:split], total[split:] + rv[2, split:].astype(F32)], axis=0)
            self.sv[5] = total.astype(BF16)
            self.last.append(self.deliver(5, 2))
            self.r2.wait_recv()
            self.r4a.wait_recv()
            total = self.pair_sum(6) + rv[1].astype(F32)
            total = jnp.concatenate([total[0:split] + rv[2, 0:split].astype(F32), total[split:]], axis=0)
            self.sv[6] = total.astype(BF16)
            self.last.append(self.deliver(6, -2))

        def final(self):
            for copy in self.last:
                copy.wait_recv()
            total = self.rv[7].astype(F32) if self.back else self.pair_sum(7)
            for n in (3, 4, 5, 6):
                total = total + self.rv[n].astype(F32)
            return total

    class RowScatter:
        def compute(self):
            self.sib = send(gt.at[:, other], gts, sibling)

        def row(self, n, offset):
            return send(gtv.at[n : n + 1], gtr.at[n : n + 1], chip(offset))

        def stage_one(self):
            self.sib.wait_recv()
            gtv[...] = gt[:, mine] + gts[...]
            self.inner = [self.row(0, 1), self.row(1, -1), self.row(2, -2)]
            self.last = [self.row(3, 1), self.row(4, -1)]

        def stage_two(self):
            for copy in self.inner:
                copy.wait_recv()
            gtv[5:6] = gtv[5:6] + gtr[0:1]
            gtv[6:7] = gtv[6:7] + gtr[1:2] + gtr[2:3]
            self.last += [self.row(5, 2), self.row(6, -2)]

        def final(self):
            for copy in self.last:
                copy.wait_recv()
            return gtv[7:8] + gtr[3:4] + gtr[4:5] + gtr[5:6] + gtr[6:7]

    ga_s0 = Gather(g0, TOK + RANK, 48, lead=gn)
    ga_t0 = Gather(g1, TOK, 32)
    ga_s1 = Gather(g2, TOK, 32)
    ga_t1 = Gather(g3, TOK, 32)
    rs0 = Scatter(TOK, 32, pb0, sb0, sv0, rv0, True)
    rs1 = Scatter(TOK + RANK, 48, pb1, sb1, sv1, rv1, False)
    rows = RowScatter()

    def fresh():
        return jnp.zeros((TOK, 128), F32), jnp.zeros((TOK, COLS), F32)

    l_s0.wait()
    l_a.wait()
    ga_s0.begin()
    l_tg.wait()
    early_cot = send(tg, tgx, previous(0), has_previous)
    l_fz.wait()
    l_p.wait()
    norms = jnp.zeros((8, COLS), F32)
    squares = jnp.zeros((TOK, 128), F32)
    total = jnp.zeros((TOK + RANK, COLS), F32)
    ga_s0.ready(0)
    norms = build(0, norms)
    squares, total = chunk(g0, 0, squares, total, True)
    ga_s0.pass_on()
    l_t0.wait()
    ga_t0.begin()
    ga_s0.share_near()
    for slot in (6, 2, 7, 1):
        ga_s0.ready(slot)
        norms = build(slot, norms)
        squares, total = chunk(g0, slot, squares, total, True)
    ga_s0.share_far()
    ga_t0.pass_on()
    l_s1.wait()
    ga_s1.begin()
    for slot in (5, 3, 4):
        ga_s0.ready(slot)
        norms = build(slot, norms)
        squares, total = chunk(g0, slot, squares, total, True)
    norm_squares = jnp.sum(norms, axis=0, keepdims=True) + 1e-06
    colnorm = jnp.sqrt(norm_squares)
    col_scale = mag_ref[...] / colnorm
    r0 = rscale_of(squares)
    raw0 = total[0:TOK] * r0
    adapter_direction = total[TOK:]
    preact = raw0 * col_scale
    pg = tg[...].astype(F32) * slope_of(preact)
    pgs0 = (pg * col_scale).astype(BF16)
    inner = jnp.sum(pg * raw0, axis=0, keepdims=True)
    rs0.prepare(pgs0, g0, r0, jnp.sum(pg * preact, axis=1, keepdims=True))
    rs0.compute_first()
    rs0.compute_second()
    ga_t0.share_near()
    ga_s1.pass_on()
    rs0.stage_one()
    ga_t0.share_far()
    squares, total = fresh()
    for slot in (0, 6, 2, 7, 1):
        ga_t0.ready(slot)
        squares, total = chunk(g1, slot, squares, total)
    rs0.stage_one_direct()
    for slot in (5, 3, 4):
        ga_t0.ready(slot)
        squares, total = chunk(g1, slot, squares, total)
    preact = total * rscale_of(squares) * col_scale
    em[...] = (g1[0, :, mine].astype(F32) + preact / (1.0 + jnp.exp(-preact))).astype(BF16)
    l_ent.wait()
    ga_t1.begin_next(em, ent)
    ga_s1.share_near()
    rs0.stage_two()
    normalise(g0, zn0, r0)
    factor = aout[...]
    weights0 = dot_nt(factor, pgs0)
    ga_s1.share_far()
    squares1, total1 = fresh()
    for slot in (0, 6, 2, 7, 1):
        ga_s1.ready(slot)
        squares1, total1 = chunk(g2, slot, squares1, total1)
    for slot in (5, 3, 4):
        ga_s1.ready(slot)
        squares1, total1 = chunk(g2, slot, squares1, total1)
    r1 = rscale_of(squares1)
    raw1 = total1 * r1
    preact1 = raw1 * col_scale
    slope = slope_of(preact1)
    normalise(g2, zn1, r1)
    ga_t1.share_own(ent)
    ga_t1.pass_on()
    l_ret.wait()

    @pl.when(has_following)
    def _():
        early_cot.wait_recv()
        gx[...] = (tgx[...].astype(F32) + rs0.final()).astype(BF16)

    @pl.when(jnp.logical_not(has_following))
    def _():
        gx[...] = ret[...]

    cot1 = gx[...].astype(F32)
    pg = cot1 * slope
    pgs1 = (pg * col_scale).astype(BF16)
    inner = inner + jnp.sum(pg * raw1, axis=0, keepdims=True)
    scaled_ratio = col_scale * inner / norm_squares
    weights = jnp.concatenate([weights0, dot_nt(factor, pgs1)], axis=1).astype(BF16)
    shrunk = (factor.astype(F32) * -scaled_ratio).astype(BF16)

    def column_extra(slot):
        return dot(weights, jnp.concatenate([zn0[slot], zn1[slot]], axis=0))

    rs1.prepare(
        jnp.concatenate([pgs1, shrunk], axis=0), g2, r1, jnp.sum(pg * preact1, axis=1, keepdims=True), column_extra
    )
    rs1.compute_first()
    rs1.compute_second()
    rows.compute()
    rs1.stage_one()
    rs1.stage_one_direct()
    rows.stage_one()
    ga_t1.share_near()
    mag_o[...] = inner / colnorm
    product = jnp.zeros((RANK, TOK * SLOTS), F32)
    for slot in range(CHIPS):
        product = product + dot_nt(
            g0[slot, TOK : TOK + RANK, :], jnp.concatenate([zn0[slot], zn1[slot]], axis=0)
        )
    upper = product.astype(BF16)
    lower = (product - upper.astype(F32)).astype(BF16)
    both = dot(jnp.concatenate([upper, lower], axis=0), jnp.concatenate([pgs0, pgs1], axis=0))
    gout_o[0] = both[0:RANK] + both[RANK:] - adapter_direction * scaled_ratio
    squares, total = fresh()
    for slot in (0, 6, 2, 7, 1):
        ga_t1.ready(slot)
        squares, total = chunk(g3, slot, squares, total)
    ga_t1.share_far()
    rs1.stage_two()
    rows.stage_two()
    for slot in (5, 3, 4):
        ga_t1.ready(slot)
        squares, total = chunk(g3, slot, squares, total)
    preact = total * rscale_of(squares) * col_scale
    act_o[0] = g3[0, :, mine].astype(F32) + preact / (1.0 + jnp.exp(-preact))
    gain_o[...] = rows.final()
    result = rs1.final()
    gin_o[0] = result[TOK:]
    grad_o[0] = cot1 + result[0:TOK]
    for copy, condition in started:
        if condition is None:
            copy.wait_send()
        else:
            pl.when(condition)(copy.wait_send)


def local(*args):
    hbm = pl.BlockSpec(memory_space=pltpu.HBM)
    vmem = pl.BlockSpec(memory_space=pltpu.VMEM)
    rows1 = TOK + RANK

    def scatter_buffers(rows):
        return [
            pltpu.VMEM((8, rows, PAIR), BF16),
            pltpu.VMEM((8, rows, COLS), BF16),
            pltpu.VMEM((8, rows, COLS), BF16),
            pltpu.VMEM((8, rows, COLS), BF16),
        ]

    gathered = pltpu.VMEM((CHIPS, TOK, PAIR), BF16)
    block = pltpu.VMEM((TOK, COLS), BF16)
    out_shape = (
        jax.ShapeDtypeStruct((1, TOK, COLS), F32),
        jax.ShapeDtypeStruct((1, TOK, COLS), F32),
        jax.ShapeDtypeStruct((1, COLS), F32),
        jax.ShapeDtypeStruct((1, RANK, COLS), F32),
        jax.ShapeDtypeStruct((1, RANK, COLS), F32),
        jax.ShapeDtypeStruct((1, COLS), F32),
    )
    act, grad, *sums = pl.pallas_call(
        kernel,
        out_shape=out_shape,
        in_specs=[hbm] * 8 + [vmem] * 2,
        out_specs=(vmem,) * 6,
        scratch_shapes=[
            pltpu.VMEM((FEATURES, COLS), BF16),
            pltpu.VMEM((FEATURES, COLS), BF16),
            pltpu.VMEM((CHIPS, rows1, PAIR), BF16),
            gathered,
            gathered,
            gathered,
            pltpu.VMEM((CHIPS, 8, PAIR), F32),
            gathered,
            gathered,
            block,
            block,
            block,
            block,
            pltpu.VMEM((RANK, COLS), BF16),
            block,
            block,
            *scatter_buffers(TOK),
            *scatter_buffers(rows1),
            pltpu.VMEM((8, PAIR), F32),
            pltpu.VMEM((8, COLS), F32),
            pltpu.VMEM((8, COLS), F32),
            pltpu.VMEM((8, COLS), F32),
            pltpu.SemaphoreType.DMA((COPIES,)),
            pltpu.SemaphoreType.DMA((COPIES,)),
            pltpu.SemaphoreType.DMA((9,)),
        ],
        compiler_params=pltpu.CompilerParams(
            collective_id=0, has_side_effects=True, vmem_limit_bytes=56 * 2**20
        ),
        name="window",
    )(*args)
    mean = 1.0 / (SLOTS * TOK)
    return act.astype(BF16), grad.astype(BF16), *[total * mean for total in sums]


def solution(mesh):
    in_specs = (
        P("section", None, "tensor"),
        P(None, None, "tensor"),
        P("section", None, None, "tensor"),
        P("section", None, "tensor"),
        P(None, None, "tensor"),
        P("section", None, "tensor"),
        P("section", None, "tensor"),
        P("section", None, "tensor"),
        P("section", "tensor"),
        P("section", "tensor"),
    )
    out_specs = (
        P("section", None, "tensor"),
        P("section", None, "tensor"),
        P("section", "tensor"),
        P("section", None, "tensor"),
        P("section", None, "tensor"),
        P("section", "tensor"),
    )
    return jax.shard_map(local, mesh=mesh, in_specs=in_specs, out_specs=out_specs, check_vma=False)
```

```python
import math

import jax
import jax.numpy as jnp
from jax import lax
from jax.experimental import pallas as pl
from jax.experimental.pallas import tpu as pltpu
from jax.sharding import PartitionSpec as P

F32 = jnp.float32
BF16 = jnp.bfloat16
MESH = pl.DeviceIdType.MESH
CHIPS = 8
TOK = 64
RANK = 16
COLS = 384
PAIR = 2 * COLS
FEATURES = CHIPS * PAIR
SLOTS = 2
ORDER = (3, 5, 4, 1, 7, 2, 6, 0)
ARRIVALS = 90
DEPARTURES = 30


def dot(a, b):
    return jnp.dot(a, b, preferred_element_type=F32)


def dot_nt(a, b):
    return lax.dot_general(a, b, (((1,), (1,)), ((), ())), preferred_element_type=F32)


def dot_tn(a, b):
    return lax.dot_general(a, b, (((0,), (0,)), ((), ())), preferred_element_type=F32)


def lane_groups(x):
    total = x[:, 0:128]
    for start in range(128, x.shape[1], 128):
        total = total + x[:, start : start + 128]
    return total


def kernel(
    act_hbm, ent_hbm, sta_hbm, tg_hbm, ret_hbm, frozen_hbm, ain_hbm, aout_hbm, mag_ref, gain_ref,
    packed,
    fz, w, g0, g1, g2, g3, gn, zn0, zn1, tg, tgx, ent, ret, aout, em, gx,
    pb0, sb0, sv0, rv0, pb1, sb1, sv1, rv1, gt, gts, gtv, gtr, ssem, rsem, lsem,
):
    me = lax.axis_index("tensor")
    sec = lax.axis_index("section")
    sections = lax.axis_size("section")
    y = me // 2
    core = me - 2 * y
    mine = pl.ds(pl.multiple_of(core * COLS, 128), COLS)
    other = pl.ds(pl.multiple_of((1 - core) * COLS, 128), COLS)

    def chip(offset):
        return {"tensor": lax.rem(y + offset + CHIPS, CHIPS) * 2 + core}

    def previous(offset):
        return {"section": sec - 1, **chip(offset)}

    def following(offset):
        return {"section": sec + 1, **chip(offset)}

    sibling = {"tensor": me + 1 - 2 * core}
    has_previous = sec > 0
    has_following = sec < sections - 1
    no_previous = jnp.logical_not(has_previous)
    conditions = (None, has_previous, has_following, no_previous)

    arrivals = [0]
    departures = [4]
    sent = [0, 0, 0, 0]
    alone = []

    class Arrival:
        def __init__(self, ref):
            self.ref, self.index, self.waited = ref, arrivals[0], False
            arrivals[0] += 1

        def wait(self):
            if not self.waited:
                pltpu.make_async_copy(self.ref, self.ref, rsem.at[self.index]).wait()
            self.waited = True

    def send(src, dst, device, arrival=None, kind=0):
        arrival = Arrival(dst) if arrival is None else arrival
        if kind is None:
            index = departures[0]
            departures[0] += 1
        else:
            index = kind
            sent[kind] += math.prod(src.shape) // COLS
        copy = pltpu.make_async_remote_copy(
            src_ref=src, dst_ref=dst, send_sem=ssem.at[index], recv_sem=rsem.at[arrival.index],
            device_id=device, device_id_type=MESH,
        )
        if kind is None:
            alone.append(copy)
        if kind:
            pl.when(conditions[kind])(copy.start)
        else:
            copy.start()
        return arrival

    locals_ = []

    def load(src, dst):
        copy = pltpu.make_async_copy(src, dst, lsem.at[len(locals_)])
        copy.start()
        locals_.append(copy)
        return copy

    l_s0 = load(sta_hbm.at[0, 0], g0.at[0, 0:TOK, mine])
    l_a = load(ain_hbm.at[0], g0.at[0, TOK : TOK + RANK, mine])
    l_fz = load(frozen_hbm.at[0], fz)
    l_p = load(aout_hbm.at[0], aout)
    l_t0 = load(act_hbm.at[0], g1.at[0, :, mine])
    l_tg = load(tg_hbm.at[0], tg)
    l_s1 = load(sta_hbm.at[0, 1], g2.at[0, :, mine])
    l_ent = load(ent_hbm.at[0], ent)
    l_ret = load(ret_hbm.at[0], ret)

    barrier = pltpu.get_barrier_semaphore()
    near = (0, 1, -1, 2, -2)

    def greet(peers):
        for peer in peers:
            pl.semaphore_signal(barrier, inc=1, device_id=peer, device_id_type=MESH)

    greet([chip(offset) for offset in near[1:]] + [sibling])

    @pl.when(has_previous)
    def _():
        greet([previous(offset) for offset in near])

    @pl.when(has_following)
    def _():
        greet([following(offset) for offset in near])

    gain = gain_ref[...].astype(F32)
    gn[0, 0:1, mine] = gain
    expected = len(near) * (1 + jnp.where(has_following, 1, 0) + jnp.where(has_previous, 1, 0))
    pl.semaphore_wait(barrier, expected)

    class Gather:
        groups = {0: (0,), 6: (6, 2), 2: (6, 2), 7: (7, 1), 1: (7, 1), 5: (5, 3, 4), 3: (5, 3, 4), 4: (5, 3, 4)}

        def __init__(self, ref, rows, split, lead=None):
            self.ref, self.rows, self.split, self.lead = ref, slice(0, rows), split, lead
            self.near, self.far, self.lead_in = {}, {}, {}
            self.far4 = Arrival(ref.at[4, self.rows, mine])
            self.shared, self.lead_shared = {}, {}
            for group in ((0,), (6, 2), (7, 1), (5, 3, 4)):
                span = slice(3, 6) if len(group) == 3 else slice(0, len(group))
                arrival = Arrival(ref.at[span, self.rows, mine])
                self.shared.update({slot: arrival for slot in group})

        def block(self, slot, rows=None):
            return self.ref.at[slot, self.rows if rows is None else rows, mine]

        def lead_row(self, slot):
            return self.lead.at[slot, 0:1, mine]

        def begin(self):
            for offset in (2, -2, 1, -1):
                slot = (-offset) % CHIPS
                if self.lead is not None:
                    self.lead_in[slot] = send(self.lead_row(0), self.lead_row(slot), chip(offset), kind=None)
                self.near[slot] = send(self.block(0), self.block(slot), chip(offset))
                if offset == 2:
                    self.share(0)

        def begin_next(self, src, first):
            for offset in (2, -2, 0, 1, -1):
                slot = (-offset) % CHIPS
                arrival = send(src, self.block(slot), following(offset), kind=2)
                if offset == 0:
                    self.own = arrival
                else:
                    self.near[slot] = arrival
                    send(first, self.block(slot), chip(offset), arrival, kind=3)

        def share_own(self, first):
            @pl.when(has_previous)
            def _():
                self.own.wait()

            @pl.when(no_previous)
            def _():
                self.ref[0, self.rows, mine] = first[...]

            self.share(0)

        def share(self, slot):
            if self.lead is not None:
                self.lead_shared[slot] = send(self.lead_row(slot), self.lead_row(slot), sibling, kind=None)
            send(self.block(slot), self.block(slot), sibling, self.shared[slot])

        def pass_on(self):
            for held, step in ((6, 1), (2, -1)):
                slot = (held - step) % CHIPS
                if self.lead is not None:
                    self.lead_in[held].wait()
                    self.lead_in[slot] = send(self.lead_row(held), self.lead_row(slot), chip(step), kind=None)
                    if step == 1:
                        self.lead_in[4] = send(self.lead_row(held), self.lead_row(4), chip(2), kind=None)
                self.near[held].wait()
                self.far[slot] = send(self.block(held), self.block(slot), chip(step))
                part = slice(0, self.split) if step == 1 else slice(self.split, self.rows.stop)
                send(self.block(held, part), self.block(4, part), chip(2 * step), self.far4)
                self.share(held)

        def share_near(self):
            for slot in (7, 1):
                self.near[slot].wait()
                if self.lead is not None:
                    self.lead_in[slot].wait()
                self.share(slot)

        def share_far(self):
            for slot in (5, 3, 4):
                (self.far4 if slot == 4 else self.far[slot]).wait()
                if self.lead is not None:
                    self.lead_in[slot].wait()
                self.share(slot)

        def ready(self, slot):
            self.shared[slot].wait()
            if self.lead is not None:
                self.lead_shared[slot].wait()

    def base_of(slot):
        return pl.multiple_of(lax.rem(y + slot, CHIPS) * PAIR, PAIR)

    def build(slot, norms):
        base = base_of(slot)
        for part in range(3):
            lanes = slice(part * 256, (part + 1) * 256)
            rows = pl.ds(pl.multiple_of(base + part * 256, 256), 256)
            direction = fz[rows, :].astype(F32) + dot_tn(g0[slot, TOK : TOK + RANK, lanes], aout[...])
            w[rows, :] = direction.astype(BF16)
            norms = norms + jnp.sum((direction * direction).reshape(32, 8, COLS), axis=0)
        return norms

    def chunk(ref, slot, squares, total, with_adapter=False):
        z = ref[slot, 0:TOK, :].astype(F32)
        squares = squares + lane_groups(z * z)
        scaled = (z * gn[slot, 0:1, :]).astype(BF16)
        if with_adapter:
            scaled = jnp.concatenate([scaled, ref[slot, TOK : TOK + RANK, :]], axis=0)
        total = total + dot(scaled, w[pl.ds(base_of(slot), PAIR), :])
        return squares, total

    def rscale_of(squares):
        return lax.rsqrt(jnp.sum(squares, axis=1, keepdims=True) / FEATURES + 1e-05)

    def normalise(ref, out, rscale):
        for slot in range(CHIPS):
            z = ref[slot, 0:TOK, :].astype(F32)
            out[slot] = (z * rscale * gn[slot, 0:1, :]).astype(BF16)

    def slope_of(preact):
        sig = 1.0 / (1.0 + jnp.exp(-preact))
        return sig * (1.0 + preact * (1.0 - sig))

    class Scatter:
        def __init__(self, rows, split, pb, sb, sv, rv, back):
            self.rows, self.split = rows, split
            self.pb, self.sb, self.sv, self.rv, self.back = pb, sb, sv, rv, back

        def prepare(self, lhs, ref, rscale, dots, extra=None):
            self.args = lhs, ref, rscale, rscale * rscale * dots / FEATURES, extra

        def compute(self, start, stop):
            lhs, ref, rscale, tilt, extra = self.args
            for n in range(start, stop):
                slot = ORDER[n]
                value = dot_nt(lhs, w[pl.ds(base_of(slot), PAIR), :])
                z = ref[slot, 0:TOK, :].astype(F32)
                scaled = value[0:TOK] * rscale
                term = jnp.sum(scaled * z, axis=0, keepdims=True)
                gt[n : n + 1, :] = term if extra is None else gt[n : n + 1, :] + term
                result = scaled * gn[slot, 0:1, :] - z * tilt
                if extra is not None:
                    result = jnp.concatenate([result, value[TOK:] + extra(slot)], axis=0)
                self.pb[n] = result.astype(BF16)
            return send(self.pb.at[start:stop, :, other], self.sb.at[start:stop], sibling)

        def compute_first(self):
            self.first = self.compute(0, 3)

        def compute_second(self):
            self.second = self.compute(3, 8)

        def pair_sum(self, n):
            return self.pb[n, :, mine].astype(F32) + self.sb[n].astype(F32)

        def deliver(self, n, offset):
            src, dst = self.sv.at[n], self.rv.at[n]
            if self.back:
                send(src, dst, previous(offset), self.last, kind=1)
            else:
                send(src, dst, chip(offset), self.last)

        def stage_one(self):
            rv, sv = self.rv, self.sv
            self.first.wait()
            sv[2] = self.pair_sum(2).astype(BF16)
            low, high = slice(0, self.split), slice(self.split, self.rows)
            self.r4a = send(sv.at[2, low], rv.at[2, low], chip(-2))
            self.r4b = send(sv.at[2, high], rv.at[2, high], chip(2))
            sv[0] = self.pair_sum(0).astype(BF16)
            self.r1 = send(sv.at[0], rv.at[0], chip(1))
            sv[1] = self.pair_sum(1).astype(BF16)
            self.r2 = send(sv.at[1], rv.at[1], chip(-1))

        def stage_one_direct(self):
            self.second.wait()
            self.last = Arrival(self.rv.at[3:8] if self.back else self.rv.at[3:7])
            for n, offset in ((3, 1), (4, -1)):
                self.sv[n] = self.pair_sum(n).astype(BF16)
                self.deliver(n, offset)
            if self.back:
                self.sv[7] = self.pair_sum(7).astype(BF16)
                self.deliver(7, 0)

        def stage_two(self):
            rv, split = self.rv, self.split
            self.r1.wait()
            self.r4b.wait()
            total = self.pair_sum(5) + rv[0].astype(F32)
            total = jnp.concatenate([total[0:split], total[split:] + rv[2, split:].astype(F32)], axis=0)
            self.sv[5] = total.astype(BF16)
            self.deliver(5, 2)
            self.r2.wait()
            self.r4a.wait()
            total = self.pair_sum(6) + rv[1].astype(F32)
            total = jnp.concatenate([total[0:split] + rv[2, 0:split].astype(F32), total[split:]], axis=0)
            self.sv[6] = total.astype(BF16)
            self.deliver(6, -2)

        def final(self):
            self.last.wait()
            total = self.rv[7].astype(F32) if self.back else self.pair_sum(7)
            for n in (3, 4, 5, 6):
                total = total + self.rv[n].astype(F32)
            return total

    class RowScatter:
        def compute(self):
            self.sib = send(gt.at[:, other], gts, sibling, kind=None)

        def row(self, n, offset):
            return send(gtv.at[n : n + 1], gtr.at[n : n + 1], chip(offset), kind=None)

        def stage_one(self):
            self.sib.wait()
            gtv[...] = gt[:, mine] + gts[...]
            self.inner = [self.row(0, 1), self.row(1, -1), self.row(2, -2)]
            self.last = [self.row(3, 1), self.row(4, -1)]

        def stage_two(self):
            for copy in self.inner:
                copy.wait()
            gtv[5:6] = gtv[5:6] + gtr[0:1]
            gtv[6:7] = gtv[6:7] + gtr[1:2] + gtr[2:3]
            self.last += [self.row(5, 2), self.row(6, -2)]

        def final(self):
            for copy in self.last:
                copy.wait()
            return gtv[7:8] + gtr[3:4] + gtr[4:5] + gtr[5:6] + gtr[6:7]

    ga_s0 = Gather(g0, TOK + RANK, 48, lead=gn)
    ga_t0 = Gather(g1, TOK, 32)
    ga_s1 = Gather(g2, TOK, 32)
    ga_t1 = Gather(g3, TOK, 32)
    rs0 = Scatter(TOK, 32, pb0, sb0, sv0, rv0, True)
    rs1 = Scatter(TOK + RANK, 48, pb1, sb1, sv1, rv1, False)
    rows = RowScatter()

    def fresh():
        return jnp.zeros((TOK, 128), F32), jnp.zeros((TOK, COLS), F32)

    l_s0.wait()
    l_a.wait()
    ga_s0.begin()
    l_tg.wait()
    early_cot = send(tg, tgx, previous(0), kind=1)
    l_fz.wait()
    l_p.wait()
    norms = jnp.zeros((8, COLS), F32)
    squares = jnp.zeros((TOK, 128), F32)
    total = jnp.zeros((TOK + RANK, COLS), F32)
    ga_s0.ready(0)
    norms = build(0, norms)
    squares, total = chunk(g0, 0, squares, total, True)
    ga_s0.pass_on()
    l_t0.wait()
    ga_t0.begin()
    ga_s0.share_near()
    for slot in (6, 2, 7, 1):
        ga_s0.ready(slot)
        norms = build(slot, norms)
        squares, total = chunk(g0, slot, squares, total, True)
    ga_s0.share_far()
    ga_t0.pass_on()
    l_s1.wait()
    ga_s1.begin()
    for slot in (5, 3, 4):
        ga_s0.ready(slot)
        norms = build(slot, norms)
        squares, total = chunk(g0, slot, squares, total, True)
    norm_squares = jnp.sum(norms, axis=0, keepdims=True) + 1e-06
    colnorm = jnp.sqrt(norm_squares)
    col_scale = mag_ref[...] / colnorm
    r0 = rscale_of(squares)
    raw0 = total[0:TOK] * r0
    adapter_direction = total[TOK:]
    preact = raw0 * col_scale
    pg = tg[...].astype(F32) * slope_of(preact)
    pgs0 = (pg * col_scale).astype(BF16)
    inner = jnp.sum(pg * raw0, axis=0, keepdims=True)
    rs0.prepare(pgs0, g0, r0, jnp.sum(pg * preact, axis=1, keepdims=True))
    rs0.compute_first()
    rs0.compute_second()
    ga_t0.share_near()
    ga_s1.pass_on()
    rs0.stage_one()
    ga_t0.share_far()
    squares, total = fresh()
    for slot in (0, 6, 2, 7, 1):
        ga_t0.ready(slot)
        squares, total = chunk(g1, slot, squares, total)
    rs0.stage_one_direct()
    for slot in (5, 3, 4):
        ga_t0.ready(slot)
        squares, total = chunk(g1, slot, squares, total)
    preact = total * rscale_of(squares) * col_scale
    em[...] = (g1[0, :, mine].astype(F32) + preact / (1.0 + jnp.exp(-preact))).astype(BF16)
    l_ent.wait()
    ga_t1.begin_next(em, ent)
    ga_s1.share_near()
    rs0.stage_two()
    normalise(g0, zn0, r0)
    factor = aout[...]
    weights0 = dot_nt(factor, pgs0)
    ga_s1.share_far()
    squares1, total1 = fresh()
    for slot in (0, 6, 2, 7, 1):
        ga_s1.ready(slot)
        squares1, total1 = chunk(g2, slot, squares1, total1)
    for slot in (5, 3, 4):
        ga_s1.ready(slot)
        squares1, total1 = chunk(g2, slot, squares1, total1)
    r1 = rscale_of(squares1)
    raw1 = total1 * r1
    preact1 = raw1 * col_scale
    slope = slope_of(preact1)
    normalise(g2, zn1, r1)
    ga_t1.share_own(ent)
    ga_t1.pass_on()
    l_ret.wait()

    @pl.when(has_following)
    def _():
        early_cot.wait()
        gx[...] = (tgx[...].astype(F32) + rs0.final()).astype(BF16)

    @pl.when(jnp.logical_not(has_following))
    def _():
        gx[...] = ret[...]

    cot1 = gx[...].astype(F32)
    pg = cot1 * slope
    pgs1 = (pg * col_scale).astype(BF16)
    inner = inner + jnp.sum(pg * raw1, axis=0, keepdims=True)
    scaled_ratio = col_scale * inner / norm_squares
    weights = jnp.concatenate([weights0, dot_nt(factor, pgs1)], axis=1).astype(BF16)
    shrunk = (factor.astype(F32) * -scaled_ratio).astype(BF16)

    def column_extra(slot):
        return dot(weights, jnp.concatenate([zn0[slot], zn1[slot]], axis=0))

    rs1.prepare(
        jnp.concatenate([pgs1, shrunk], axis=0), g2, r1, jnp.sum(pg * preact1, axis=1, keepdims=True), column_extra
    )
    rs1.compute_first()
    rs1.compute_second()
    rows.compute()
    rs1.stage_one()
    rs1.stage_one_direct()
    rows.stage_one()
    ga_t1.share_near()
    packed[160:168] = jnp.zeros((8, COLS), F32)
    packed[160:161] = inner / colnorm
    product = jnp.zeros((RANK, TOK * SLOTS), F32)
    for slot in range(CHIPS):
        product = product + dot_nt(
            g0[slot, TOK : TOK + RANK, :], jnp.concatenate([zn0[slot], zn1[slot]], axis=0)
        )
    upper = product.astype(BF16)
    lower = (product - upper.astype(F32)).astype(BF16)
    both = dot(jnp.concatenate([upper, lower], axis=0), jnp.concatenate([pgs0, pgs1], axis=0))
    packed[144:160] = both[0:RANK] + both[RANK:] - adapter_direction * scaled_ratio
    squares, total = fresh()
    for slot in (0, 6, 2, 7, 1):
        ga_t1.ready(slot)
        squares, total = chunk(g3, slot, squares, total)
    ga_t1.share_far()
    rs1.stage_two()
    rows.stage_two()
    for slot in (5, 3, 4):
        ga_t1.ready(slot)
        squares, total = chunk(g3, slot, squares, total)
    preact = total * rscale_of(squares) * col_scale
    packed[0:64] = g3[0, :, mine].astype(F32) + preact / (1.0 + jnp.exp(-preact))
    packed[161:162] = rows.final()
    result = rs1.final()
    packed[128:144] = result[TOK:]
    packed[64:128] = cot1 + result[0:TOK]
    for copy in alone:
        copy.wait_send()
    for kind, condition in enumerate(conditions):
        everything = w.at[0 : sent[kind]]
        copy = pltpu.make_async_copy(everything, everything, ssem.at[kind])
        if condition is None:
            copy.wait()
        else:
            pl.when(condition)(copy.wait)


def hand_out(packed, act, grad, mag, grad_in, grad_out, gain):
    mean = 1.0 / (SLOTS * TOK)
    act[0] = packed[0:64].astype(BF16)
    grad[0] = packed[64:128].astype(BF16)
    grad_in[0] = packed[128:144] * mean
    grad_out[0] = packed[144:160] * mean
    mag[...] = packed[160:161] * mean
    gain[...] = packed[161:162] * mean


def local(*args):
    hbm = pl.BlockSpec(memory_space=pltpu.HBM)
    vmem = pl.BlockSpec(memory_space=pltpu.VMEM)
    rows1 = TOK + RANK

    def scatter_buffers(rows):
        return [
            pltpu.VMEM((8, rows, PAIR), BF16),
            pltpu.VMEM((8, rows, COLS), BF16),
            pltpu.VMEM((8, rows, COLS), BF16),
            pltpu.VMEM((8, rows, COLS), BF16),
        ]

    gathered = pltpu.VMEM((CHIPS, TOK, PAIR), BF16)
    block = pltpu.VMEM((TOK, COLS), BF16)
    out_shape = (
        jax.ShapeDtypeStruct((1, TOK, COLS), BF16),
        jax.ShapeDtypeStruct((1, TOK, COLS), BF16),
        jax.ShapeDtypeStruct((1, COLS), F32),
        jax.ShapeDtypeStruct((1, RANK, COLS), F32),
        jax.ShapeDtypeStruct((1, RANK, COLS), F32),
        jax.ShapeDtypeStruct((1, COLS), F32),
    )
    packed = pl.pallas_call(
        kernel,
        out_shape=jax.ShapeDtypeStruct((168, COLS), F32),
        in_specs=[hbm] * 8 + [vmem] * 2,
        out_specs=vmem,
        scratch_shapes=[
            pltpu.VMEM((FEATURES, COLS), BF16),
            pltpu.VMEM((FEATURES, COLS), BF16),
            pltpu.VMEM((CHIPS, rows1, PAIR), BF16),
            gathered,
            gathered,
            gathered,
            pltpu.VMEM((CHIPS, 8, PAIR), F32),
            gathered,
            gathered,
            block,
            block,
            block,
            block,
            pltpu.VMEM((RANK, COLS), BF16),
            block,
            block,
            *scatter_buffers(TOK),
            *scatter_buffers(rows1),
            pltpu.VMEM((8, PAIR), F32),
            pltpu.VMEM((8, COLS), F32),
            pltpu.VMEM((8, COLS), F32),
            pltpu.VMEM((8, COLS), F32),
            pltpu.SemaphoreType.DMA((DEPARTURES,)),
            pltpu.SemaphoreType.DMA((ARRIVALS,)),
            pltpu.SemaphoreType.DMA((9,)),
        ],
        compiler_params=pltpu.CompilerParams(
            collective_id=0, has_side_effects=True, vmem_limit_bytes=56 * 2**20
        ),
        name="window",
    )(*args)
    return pl.pallas_call(
        hand_out, out_shape=out_shape, in_specs=[vmem], out_specs=(vmem,) * 6, name="hand_out"
    )(packed)


def solution(mesh):
    in_specs = (
        P("section", None, "tensor"),
        P(None, None, "tensor"),
        P("section", None, None, "tensor"),
        P("section", None, "tensor"),
        P(None, None, "tensor"),
        P("section", None, "tensor"),
        P("section", None, "tensor"),
        P("section", None, "tensor"),
        P("section", "tensor"),
        P("section", "tensor"),
    )
    out_specs = (
        P("section", None, "tensor"),
        P("section", None, "tensor"),
        P("section", "tensor"),
        P("section", None, "tensor"),
        P("section", None, "tensor"),
        P("section", "tensor"),
    )
    return jax.shard_map(local, mesh=mesh, in_specs=in_specs, out_specs=out_specs, check_vma=False)
```

```python
import math

import jax
import jax.numpy as jnp
from jax import lax
from jax.experimental import pallas as pl
from jax.experimental.pallas import tpu as pltpu
from jax.sharding import PartitionSpec as P

F32 = jnp.float32
BF16 = jnp.bfloat16
MESH = pl.DeviceIdType.MESH
CHIPS = 8
TOK = 64
RANK = 16
COLS = 384
PAIR = 2 * COLS
FEATURES = CHIPS * PAIR
SLOTS = 2
ORDER = (3, 5, 4, 1, 7, 2, 6, 0)
ARRIVALS = 94
DEPARTURES = 30


def dot(a, b):
    return jnp.dot(a, b, preferred_element_type=F32)


def dot_nt(a, b):
    return lax.dot_general(a, b, (((1,), (1,)), ((), ())), preferred_element_type=F32)


def dot_tn(a, b):
    return lax.dot_general(a, b, (((0,), (0,)), ((), ())), preferred_element_type=F32)


def lane_groups(x):
    total = x[:, 0:128]
    for start in range(128, x.shape[1], 128):
        total = total + x[:, start : start + 128]
    return total


def kernel(
    act_hbm, ent_hbm, sta_hbm, tg_hbm, ret_hbm, frozen_hbm, ain_hbm, aout_hbm, mag_ref, gain_ref,
    packed,
    fz, w, g0, g1, g2, g3, gn, zn0, zn1, tg, tgx, ent, ret, aout, em, gx,
    pb0, sb0, sv0, rv0, pb1, sb1, sv1, rv1, gt, gts, gtv, gtr, ssem, rsem, lsem,
):
    me = lax.axis_index("tensor")
    sec = lax.axis_index("section")
    sections = lax.axis_size("section")
    y = me // 2
    core = me - 2 * y
    mine = pl.ds(pl.multiple_of(core * COLS, 128), COLS)
    other = pl.ds(pl.multiple_of((1 - core) * COLS, 128), COLS)

    def chip(offset):
        return {"tensor": lax.rem(y + offset + CHIPS, CHIPS) * 2 + core}

    def previous(offset):
        return {"section": sec - 1, **chip(offset)}

    def following(offset):
        return {"section": sec + 1, **chip(offset)}

    sibling = {"tensor": me + 1 - 2 * core}
    has_previous = sec > 0
    has_following = sec < sections - 1
    no_previous = jnp.logical_not(has_previous)
    conditions = (None, has_previous, has_following, no_previous)

    arrivals = [0]
    departures = [4]
    sent = [0, 0, 0, 0]
    alone = []

    class Arrival:
        def __init__(self, ref):
            self.ref, self.index, self.waited = ref, arrivals[0], False
            arrivals[0] += 1

        def wait(self):
            if not self.waited:
                pltpu.make_async_copy(self.ref, self.ref, rsem.at[self.index]).wait()
            self.waited = True

    def send(src, dst, device, arrival=None, kind=0):
        arrival = Arrival(dst) if arrival is None else arrival
        if kind is None:
            index = departures[0]
            departures[0] += 1
        else:
            index = kind
            sent[kind] += math.prod(src.shape) // COLS
        copy = pltpu.make_async_remote_copy(
            src_ref=src, dst_ref=dst, send_sem=ssem.at[index], recv_sem=rsem.at[arrival.index],
            device_id=device, device_id_type=MESH,
        )
        if kind is None:
            alone.append(copy)
        if kind:
            pl.when(conditions[kind])(copy.start)
        else:
            copy.start()
        return arrival

    locals_ = []

    def load(src, dst):
        copy = pltpu.make_async_copy(src, dst, lsem.at[len(locals_)])
        copy.start()
        locals_.append(copy)
        return copy

    l_s0 = load(sta_hbm.at[0, 0], g0.at[0, 0:TOK, mine])
    l_a = load(ain_hbm.at[0], g0.at[0, TOK : TOK + RANK, mine])
    l_fz = load(frozen_hbm.at[0], fz)
    l_p = load(aout_hbm.at[0], aout)
    l_t0 = load(act_hbm.at[0], g1.at[0, :, mine])
    l_tg = load(tg_hbm.at[0], tg)
    l_s1 = load(sta_hbm.at[0, 1], g2.at[0, :, mine])
    l_ent = load(ent_hbm.at[0], ent)
    l_ret = load(ret_hbm.at[0], ret)

    barrier = pltpu.get_barrier_semaphore()
    near = (0, 1, -1, 2, -2)

    def greet(peers):
        for peer in peers:
            pl.semaphore_signal(barrier, inc=1, device_id=peer, device_id_type=MESH)

    greet([chip(offset) for offset in near[1:]] + [sibling])

    @pl.when(has_previous)
    def _():
        greet([previous(offset) for offset in near])

    @pl.when(has_following)
    def _():
        greet([following(offset) for offset in near])

    gain = gain_ref[...].astype(F32)
    gn[0, 0:1, mine] = gain
    expected = len(near) * (1 + jnp.where(has_following, 1, 0) + jnp.where(has_previous, 1, 0))
    pl.semaphore_wait(barrier, expected)

    class Gather:
        groups = {0: (0,), 6: (6, 2), 2: (6, 2), 7: (7, 1), 1: (7, 1), 5: (5, 3, 4), 3: (5, 3, 4), 4: (5, 3, 4)}

        def __init__(self, ref, rows, split, lead=None, deep=False):
            self.ref, self.rows, self.split, self.lead, self.deep = ref, slice(0, rows), split, lead, deep
            self.near, self.far, self.lead_in = {}, {}, {}
            self.far4 = Arrival(ref.at[4, self.rows, mine])
            self.shared, self.lead_shared = {}, {}
            for group in ((0,), (6, 2), (7, 1), (5, 3, 4)):
                span = slice(3, 6) if len(group) == 3 else slice(0, len(group))
                arrival = Arrival(ref.at[span, self.rows, mine])
                self.shared.update({slot: arrival for slot in group})

        def block(self, slot, rows=None):
            return self.ref.at[slot, self.rows if rows is None else rows, mine]

        def lead_row(self, slot):
            return self.lead.at[slot, 0:1, mine]

        def begin(self, offsets=(2, -2, 1, -1)):
            for offset in offsets:
                slot = (-offset) % CHIPS
                if self.lead is not None:
                    self.lead_in[slot] = send(self.lead_row(0), self.lead_row(slot), chip(offset), kind=None)
                self.near[slot] = send(self.block(0), self.block(slot), chip(offset))
                if offset == 2:
                    self.share(0)

        def begin_next(self, src, first):
            for offset in (0, 1, -1) if self.deep else (2, -2, 0, 1, -1):
                slot = (-offset) % CHIPS
                arrival = send(src, self.block(slot), following(offset), kind=2)
                if offset == 0:
                    self.own = arrival
                else:
                    self.near[slot] = arrival
                    send(first, self.block(slot), chip(offset), arrival, kind=3)

        def share_own(self, first):
            @pl.when(has_previous)
            def _():
                self.own.wait()

            @pl.when(no_previous)
            def _():
                self.ref[0, self.rows, mine] = first[...]

            self.share(0)

        def share(self, slot):
            if self.lead is not None:
                self.lead_shared[slot] = send(self.lead_row(slot), self.lead_row(slot), sibling, kind=None)
            send(self.block(slot), self.block(slot), sibling, self.shared[slot])

        def pass_on(self):
            if self.deep:
                for held, step in ((7, 1), (1, -1)):
                    slot = (held - step) % CHIPS
                    if self.lead is not None:
                        self.lead_in[held].wait()
                        self.lead_in[slot] = send(self.lead_row(held), self.lead_row(slot), chip(step), kind=None)
                    self.near[held].wait()
                    self.near[slot] = send(self.block(held), self.block(slot), chip(step))
                    self.share(held)
            else:
                self.pass_far()

        def pass_two(self):
            if self.deep:
                self.pass_far()

        def pass_far(self):
            for held, step in ((6, 1), (2, -1)):
                slot = (held - step) % CHIPS
                if self.lead is not None:
                    self.lead_in[held].wait()
                    self.lead_in[slot] = send(self.lead_row(held), self.lead_row(slot), chip(step), kind=None)
                    if step == 1:
                        self.lead_in[4] = send(self.lead_row(held), self.lead_row(4), chip(2), kind=None)
                self.near[held].wait()
                self.far[slot] = send(self.block(held), self.block(slot), chip(step))
                part = slice(0, self.split) if step == 1 else slice(self.split, self.rows.stop)
                send(self.block(held, part), self.block(4, part), chip(2 * step), self.far4)
                self.share(held)

        def share_near(self):
            for slot in () if self.deep else (7, 1):
                self.near[slot].wait()
                if self.lead is not None:
                    self.lead_in[slot].wait()
                self.share(slot)

        def share_far(self):
            for slot in (5, 3, 4):
                (self.far4 if slot == 4 else self.far[slot]).wait()
                if self.lead is not None:
                    self.lead_in[slot].wait()
                self.share(slot)

        def ready(self, slot):
            self.shared[slot].wait()
            if self.lead is not None:
                self.lead_shared[slot].wait()

    def base_of(slot):
        return pl.multiple_of(lax.rem(y + slot, CHIPS) * PAIR, PAIR)

    def build(slot, norms):
        base = base_of(slot)
        for part in range(3):
            lanes = slice(part * 256, (part + 1) * 256)
            rows = pl.ds(pl.multiple_of(base + part * 256, 256), 256)
            direction = fz[rows, :].astype(F32) + dot_tn(g0[slot, TOK : TOK + RANK, lanes], aout[...])
            w[rows, :] = direction.astype(BF16)
            norms = norms + jnp.sum((direction * direction).reshape(32, 8, COLS), axis=0)
        return norms

    def chunk(ref, slot, squares, total, with_adapter=False):
        z = ref[slot, 0:TOK, :].astype(F32)
        squares = squares + lane_groups(z * z)
        scaled = (z * gn[slot, 0:1, :]).astype(BF16)
        if with_adapter:
            scaled = jnp.concatenate([scaled, ref[slot, TOK : TOK + RANK, :]], axis=0)
        total = total + dot(scaled, w[pl.ds(base_of(slot), PAIR), :])
        return squares, total

    def rscale_of(squares):
        return lax.rsqrt(jnp.sum(squares, axis=1, keepdims=True) / FEATURES + 1e-05)

    def normalise(ref, out, rscale):
        for slot in range(CHIPS):
            z = ref[slot, 0:TOK, :].astype(F32)
            out[slot] = (z * rscale * gn[slot, 0:1, :]).astype(BF16)

    def slope_of(preact):
        sig = 1.0 / (1.0 + jnp.exp(-preact))
        return sig * (1.0 + preact * (1.0 - sig))

    class Scatter:
        def __init__(self, rows, split, pb, sb, sv, rv, back):
            self.rows, self.split = rows, split
            self.pb, self.sb, self.sv, self.rv, self.back = pb, sb, sv, rv, back

        def prepare(self, lhs, ref, rscale, dots, extra=None):
            self.args = lhs, ref, rscale, rscale * rscale * dots / FEATURES, extra

        def compute(self, start, stop):
            lhs, ref, rscale, tilt, extra = self.args
            for n in range(start, stop):
                slot = ORDER[n]
                value = dot_nt(lhs, w[pl.ds(base_of(slot), PAIR), :])
                z = ref[slot, 0:TOK, :].astype(F32)
                scaled = value[0:TOK] * rscale
                term = jnp.sum(scaled * z, axis=0, keepdims=True)
                gt[n : n + 1, :] = term if extra is None else gt[n : n + 1, :] + term
                result = scaled * gn[slot, 0:1, :] - z * tilt
                if extra is not None:
                    result = jnp.concatenate([result, value[TOK:] + extra(slot)], axis=0)
                self.pb[n] = result.astype(BF16)
            return send(self.pb.at[start:stop, :, other], self.sb.at[start:stop], sibling)

        def part(self, start, stop):
            arrival = self.compute(start, stop)
            for n in range(start, stop):
                self.halves[n] = arrival

        def compute_first(self):
            self.halves = {}
            for n in (2, 0, 1):
                self.part(n, n + 1)
            self.part(3, 5)
            self.stage_one()

        def compute_second(self):
            self.part(5, 8)
            self.stage_one_direct()

        def pair_sum(self, n):
            return self.pb[n, :, mine].astype(F32) + self.sb[n].astype(F32)

        def deliver(self, n, offset):
            src, dst = self.sv.at[n], self.rv.at[n]
            if self.back:
                send(src, dst, previous(offset), self.last, kind=1)
            else:
                send(src, dst, chip(offset), self.last)

        def stage_one(self):
            rv, sv = self.rv, self.sv
            self.halves[2].wait()
            sv[2] = self.pair_sum(2).astype(BF16)
            low, high = slice(0, self.split), slice(self.split, self.rows)
            self.r4a = send(sv.at[2, low], rv.at[2, low], chip(-2))
            self.r4b = send(sv.at[2, high], rv.at[2, high], chip(2))
            self.halves[0].wait()
            sv[0] = self.pair_sum(0).astype(BF16)
            self.r1 = send(sv.at[0], rv.at[0], chip(1))
            self.halves[1].wait()
            sv[1] = self.pair_sum(1).astype(BF16)
            self.r2 = send(sv.at[1], rv.at[1], chip(-1))

        def stage_one_direct(self):
            self.halves[3].wait()
            self.last = Arrival(self.rv.at[3:8] if self.back else self.rv.at[3:7])
            for n, offset in ((3, 1), (4, -1)):
                self.sv[n] = self.pair_sum(n).astype(BF16)
                self.deliver(n, offset)

        def stage_two(self):
            rv, split = self.rv, self.split
            self.halves[5].wait()
            if self.back:
                self.sv[7] = self.pair_sum(7).astype(BF16)
                self.deliver(7, 0)
            self.r1.wait()
            self.r4b.wait()
            total = self.pair_sum(5) + rv[0].astype(F32)
            total = jnp.concatenate([total[0:split], total[split:] + rv[2, split:].astype(F32)], axis=0)
            self.sv[5] = total.astype(BF16)
            self.deliver(5, 2)
            self.r2.wait()
            self.r4a.wait()
            total = self.pair_sum(6) + rv[1].astype(F32)
            total = jnp.concatenate([total[0:split] + rv[2, 0:split].astype(F32), total[split:]], axis=0)
            self.sv[6] = total.astype(BF16)
            self.deliver(6, -2)

        def final(self):
            self.last.wait()
            total = self.rv[7].astype(F32) if self.back else self.pair_sum(7)
            for n in (3, 4, 5, 6):
                total = total + self.rv[n].astype(F32)
            return total

    class RowScatter:
        def compute(self):
            self.sib = send(gt.at[:, other], gts, sibling, kind=None)

        def row(self, n, offset):
            return send(gtv.at[n : n + 1], gtr.at[n : n + 1], chip(offset), kind=None)

        def stage_one(self):
            self.sib.wait()
            gtv[...] = gt[:, mine] + gts[...]
            self.inner = [self.row(0, 1), self.row(1, -1), self.row(2, -2)]
            self.last = [self.row(3, 1), self.row(4, -1)]

        def stage_two(self):
            for copy in self.inner:
                copy.wait()
            gtv[5:6] = gtv[5:6] + gtr[0:1]
            gtv[6:7] = gtv[6:7] + gtr[1:2] + gtr[2:3]
            self.last += [self.row(5, 2), self.row(6, -2)]

        def final(self):
            for copy in self.last:
                copy.wait()
            return gtv[7:8] + gtr[3:4] + gtr[4:5] + gtr[5:6] + gtr[6:7]

    ga_s0 = Gather(g0, TOK + RANK, 48, lead=gn)
    ga_t0 = Gather(g1, TOK, 32)
    ga_s1 = Gather(g2, TOK, 32)
    ga_t1 = Gather(g3, TOK, 32)
    rs0 = Scatter(TOK, 32, pb0, sb0, sv0, rv0, True)
    rs1 = Scatter(TOK + RANK, 48, pb1, sb1, sv1, rv1, False)
    rows = RowScatter()

    def fresh():
        return jnp.zeros((TOK, 128), F32), jnp.zeros((TOK, COLS), F32)

    l_s0.wait()
    l_a.wait()
    ga_s0.begin()
    l_tg.wait()
    early_cot = send(tg, tgx, previous(0), kind=1)
    l_fz.wait()
    l_p.wait()
    norms = jnp.zeros((8, COLS), F32)
    squares = jnp.zeros((TOK, 128), F32)
    total = jnp.zeros((TOK + RANK, COLS), F32)
    ga_s0.ready(0)
    norms = build(0, norms)
    squares, total = chunk(g0, 0, squares, total, True)
    ga_s0.pass_on()
    ga_s0.pass_two()
    l_t0.wait()
    ga_t0.begin()
    ga_s0.share_near()
    for slot in (6, 2, 7, 1):
        ga_s0.ready(slot)
        norms = build(slot, norms)
        squares, total = chunk(g0, slot, squares, total, True)
    ga_s0.share_far()
    ga_t0.pass_on()
    ga_t0.pass_two()
    l_s1.wait()
    ga_s1.begin()
    for slot in (5, 3, 4):
        ga_s0.ready(slot)
        norms = build(slot, norms)
        squares, total = chunk(g0, slot, squares, total, True)
    norm_squares = jnp.sum(norms, axis=0, keepdims=True) + 1e-06
    colnorm = jnp.sqrt(norm_squares)
    col_scale = mag_ref[...] / colnorm
    r0 = rscale_of(squares)
    raw0 = total[0:TOK] * r0
    adapter_direction = total[TOK:]
    preact = raw0 * col_scale
    pg = tg[...].astype(F32) * slope_of(preact)
    pgs0 = (pg * col_scale).astype(BF16)
    inner = jnp.sum(pg * raw0, axis=0, keepdims=True)
    rs0.prepare(pgs0, g0, r0, jnp.sum(pg * preact, axis=1, keepdims=True))
    rs0.compute_first()
    rs0.compute_second()
    ga_t0.share_near()
    ga_s1.pass_on()
    ga_s1.pass_two()
    ga_t0.share_far()
    squares, total = fresh()
    for slot in (0, 7, 1, 6, 2):
        ga_t0.ready(slot)
        squares, total = chunk(g1, slot, squares, total)
    rs0.stage_two()
    for slot in (5, 3, 4):
        ga_t0.ready(slot)
        squares, total = chunk(g1, slot, squares, total)
    preact = total * rscale_of(squares) * col_scale
    em[...] = (g1[0, :, mine].astype(F32) + preact / (1.0 + jnp.exp(-preact))).astype(BF16)
    l_ent.wait()
    ga_t1.begin_next(em, ent)
    ga_s1.share_near()
    normalise(g0, zn0, r0)
    factor = aout[...]
    weights0 = dot_nt(factor, pgs0)
    ga_s1.share_far()
    squares1, total1 = fresh()
    for slot in (0, 7, 1, 6, 2):
        ga_s1.ready(slot)
        squares1, total1 = chunk(g2, slot, squares1, total1)
    for slot in (5, 3, 4):
        ga_s1.ready(slot)
        squares1, total1 = chunk(g2, slot, squares1, total1)
    r1 = rscale_of(squares1)
    raw1 = total1 * r1
    preact1 = raw1 * col_scale
    slope = slope_of(preact1)
    normalise(g2, zn1, r1)
    ga_t1.share_own(ent)
    ga_t1.pass_on()
    ga_t1.pass_two()
    l_ret.wait()

    @pl.when(has_following)
    def _():
        early_cot.wait()
        gx[...] = (tgx[...].astype(F32) + rs0.final()).astype(BF16)

    @pl.when(jnp.logical_not(has_following))
    def _():
        gx[...] = ret[...]

    cot1 = gx[...].astype(F32)
    pg = cot1 * slope
    pgs1 = (pg * col_scale).astype(BF16)
    inner = inner + jnp.sum(pg * raw1, axis=0, keepdims=True)
    scaled_ratio = col_scale * inner / norm_squares
    weights = jnp.concatenate([weights0, dot_nt(factor, pgs1)], axis=1).astype(BF16)
    shrunk = (factor.astype(F32) * -scaled_ratio).astype(BF16)

    def column_extra(slot):
        return dot(weights, jnp.concatenate([zn0[slot], zn1[slot]], axis=0))

    rs1.prepare(
        jnp.concatenate([pgs1, shrunk], axis=0), g2, r1, jnp.sum(pg * preact1, axis=1, keepdims=True), column_extra
    )
    rs1.compute_first()
    rs1.compute_second()
    rows.compute()
    ga_t1.share_near()
    packed[160:168] = jnp.zeros((8, COLS), F32)
    packed[160:161] = inner / colnorm
    product = jnp.zeros((RANK, TOK * SLOTS), F32)
    for slot in range(CHIPS):
        product = product + dot_nt(
            g0[slot, TOK : TOK + RANK, :], jnp.concatenate([zn0[slot], zn1[slot]], axis=0)
        )
    upper = product.astype(BF16)
    lower = (product - upper.astype(F32)).astype(BF16)
    both = dot(jnp.concatenate([upper, lower], axis=0), jnp.concatenate([pgs0, pgs1], axis=0))
    packed[144:160] = both[0:RANK] + both[RANK:] - adapter_direction * scaled_ratio
    rows.stage_one()
    rs1.stage_two()
    rows.stage_two()
    squares, total = fresh()
    for slot in (0, 7, 1, 6, 2):
        ga_t1.ready(slot)
        squares, total = chunk(g3, slot, squares, total)
    ga_t1.share_far()
    for slot in (5, 3, 4):
        ga_t1.ready(slot)
        squares, total = chunk(g3, slot, squares, total)
    preact = total * rscale_of(squares) * col_scale
    packed[0:64] = g3[0, :, mine].astype(F32) + preact / (1.0 + jnp.exp(-preact))
    packed[161:162] = rows.final()
    result = rs1.final()
    packed[128:144] = result[TOK:]
    packed[64:128] = cot1 + result[0:TOK]
    for copy in alone:
        copy.wait_send()
    for kind, condition in enumerate(conditions):
        everything = w.at[0 : sent[kind]]
        copy = pltpu.make_async_copy(everything, everything, ssem.at[kind])
        if condition is None:
            copy.wait()
        else:
            pl.when(condition)(copy.wait)


def hand_out(packed, act, grad, mag, grad_in, grad_out, gain):
    mean = 1.0 / (SLOTS * TOK)
    act[0] = packed[0:64].astype(BF16)
    grad[0] = packed[64:128].astype(BF16)
    grad_in[0] = packed[128:144] * mean
    grad_out[0] = packed[144:160] * mean
    mag[...] = packed[160:161] * mean
    gain[...] = packed[161:162] * mean


def local(*args):
    hbm = pl.BlockSpec(memory_space=pltpu.HBM)
    vmem = pl.BlockSpec(memory_space=pltpu.VMEM)
    rows1 = TOK + RANK

    def scatter_buffers(rows):
        return [
            pltpu.VMEM((8, rows, PAIR), BF16),
            pltpu.VMEM((8, rows, COLS), BF16),
            pltpu.VMEM((8, rows, COLS), BF16),
            pltpu.VMEM((8, rows, COLS), BF16),
        ]

    gathered = pltpu.VMEM((CHIPS, TOK, PAIR), BF16)
    block = pltpu.VMEM((TOK, COLS), BF16)
    out_shape = (
        jax.ShapeDtypeStruct((1, TOK, COLS), BF16),
        jax.ShapeDtypeStruct((1, TOK, COLS), BF16),
        jax.ShapeDtypeStruct((1, COLS), F32),
        jax.ShapeDtypeStruct((1, RANK, COLS), F32),
        jax.ShapeDtypeStruct((1, RANK, COLS), F32),
        jax.ShapeDtypeStruct((1, COLS), F32),
    )
    packed = pl.pallas_call(
        kernel,
        out_shape=jax.ShapeDtypeStruct((168, COLS), F32),
        in_specs=[hbm] * 8 + [vmem] * 2,
        out_specs=vmem,
        scratch_shapes=[
            pltpu.VMEM((FEATURES, COLS), BF16),
            pltpu.VMEM((FEATURES, COLS), BF16),
            pltpu.VMEM((CHIPS, rows1, PAIR), BF16),
            gathered,
            gathered,
            gathered,
            pltpu.VMEM((CHIPS, 8, PAIR), F32),
            gathered,
            gathered,
            block,
            block,
            block,
            block,
            pltpu.VMEM((RANK, COLS), BF16),
            block,
            block,
            *scatter_buffers(TOK),
            *scatter_buffers(rows1),
            pltpu.VMEM((8, PAIR), F32),
            pltpu.VMEM((8, COLS), F32),
            pltpu.VMEM((8, COLS), F32),
            pltpu.VMEM((8, COLS), F32),
            pltpu.SemaphoreType.DMA((DEPARTURES,)),
            pltpu.SemaphoreType.DMA((ARRIVALS,)),
            pltpu.SemaphoreType.DMA((9,)),
        ],
        compiler_params=pltpu.CompilerParams(
            collective_id=0, has_side_effects=True, vmem_limit_bytes=56 * 2**20
        ),
        name="window",
    )(*args)
    return pl.pallas_call(
        hand_out, out_shape=out_shape, in_specs=[vmem], out_specs=(vmem,) * 6, name="hand_out"
    )(packed)


def solution(mesh):
    in_specs = (
        P("section", None, "tensor"),
        P(None, None, "tensor"),
        P("section", None, None, "tensor"),
        P("section", None, "tensor"),
        P(None, None, "tensor"),
        P("section", None, "tensor"),
        P("section", None, "tensor"),
        P("section", None, "tensor"),
        P("section", "tensor"),
        P("section", "tensor"),
    )
    out_specs = (
        P("section", None, "tensor"),
        P("section", None, "tensor"),
        P("section", "tensor"),
        P("section", None, "tensor"),
        P("section", None, "tensor"),
        P("section", "tensor"),
    )
    return jax.shard_map(local, mesh=mesh, in_specs=in_specs, out_specs=out_specs, check_vma=False)
```

```python
import math

import jax
import jax.numpy as jnp
from jax import lax
from jax.experimental import pallas as pl
from jax.experimental.pallas import tpu as pltpu
from jax.sharding import PartitionSpec as P

F32 = jnp.float32
BF16 = jnp.bfloat16
MESH = pl.DeviceIdType.MESH
CHIPS = 8
TOK = 64
RANK = 16
COLS = 384
PAIR = 2 * COLS
FEATURES = CHIPS * PAIR
SLOTS = 2
ORDER = (3, 5, 4, 1, 7, 2, 6, 0)
ARRIVALS = 89
DEPARTURES = 27


def dot(a, b):
    return jnp.dot(a, b, preferred_element_type=F32)


def dot_nt(a, b):
    return lax.dot_general(a, b, (((1,), (1,)), ((), ())), preferred_element_type=F32)


def dot_tn(a, b):
    return lax.dot_general(a, b, (((0,), (0,)), ((), ())), preferred_element_type=F32)


def lane_groups(x):
    total = x[:, 0:128]
    for start in range(128, x.shape[1], 128):
        total = total + x[:, start : start + 128]
    return total


def kernel(
    act_hbm, ent_hbm, sta_hbm, tg_hbm, ret_hbm, frozen_hbm, ain_hbm, aout_hbm, mag_hbm, gain_hbm,
    packed,
    mag, gain_row, fz, w, g0, g1, g2, g3, gn, zn0, zn1, tg, tgx, ent, ret, aout, em, gx,
    pb0, sb0, sv0, rv0, pb1, sb1, sv1, rv1, gt, gts, gtv, gtr, ssem, rsem, lsem,
):
    me = lax.axis_index("tensor")
    sec = lax.axis_index("section")
    sections = lax.axis_size("section")
    y = me // 2
    core = me - 2 * y
    mine = pl.ds(pl.multiple_of(core * COLS, 128), COLS)
    other = pl.ds(pl.multiple_of((1 - core) * COLS, 128), COLS)

    def chip(offset):
        return {"tensor": lax.rem(y + offset + CHIPS, CHIPS) * 2 + core}

    def previous(offset):
        return {"section": sec - 1, **chip(offset)}

    def following(offset):
        return {"section": sec + 1, **chip(offset)}

    sibling = {"tensor": me + 1 - 2 * core}
    has_previous = sec > 0
    has_following = sec < sections - 1
    no_previous = jnp.logical_not(has_previous)
    conditions = (None, has_previous, has_following, no_previous)

    arrivals = [0]
    departures = [4]
    sent = [0, 0, 0, 0]
    alone = []

    class Arrival:
        def __init__(self, ref):
            self.ref, self.index, self.waited = ref, arrivals[0], False
            arrivals[0] += 1

        def wait(self):
            if not self.waited:
                pltpu.make_async_copy(self.ref, self.ref, rsem.at[self.index]).wait()
            self.waited = True

    def send(src, dst, device, arrival=None, kind=0):
        arrival = Arrival(dst) if arrival is None else arrival
        if kind is None:
            index = departures[0]
            departures[0] += 1
        else:
            index = kind
            sent[kind] += math.prod(src.shape) // COLS
        copy = pltpu.make_async_remote_copy(
            src_ref=src, dst_ref=dst, send_sem=ssem.at[index], recv_sem=rsem.at[arrival.index],
            device_id=device, device_id_type=MESH,
        )
        if kind is None:
            alone.append(copy)
        if kind:
            pl.when(conditions[kind])(copy.start)
        else:
            copy.start()
        return arrival

    locals_ = []

    def load(src, dst):
        copy = pltpu.make_async_copy(src, dst, lsem.at[len(locals_)])
        copy.start()
        locals_.append(copy)
        return copy

    l_gain = load(gain_hbm, gain_row)
    l_mag = load(mag_hbm, mag)
    l_s0 = load(sta_hbm.at[0, 0], g0.at[0, 0:TOK, mine])
    l_a = load(ain_hbm.at[0], g0.at[0, TOK : TOK + RANK, mine])
    l_fz = load(frozen_hbm.at[0], fz)
    l_p = load(aout_hbm.at[0], aout)
    l_t0 = load(act_hbm.at[0], g1.at[0, :, mine])
    l_tg = load(tg_hbm.at[0], tg)
    l_s1 = load(sta_hbm.at[0, 1], g2.at[0, :, mine])
    l_ent = load(ent_hbm.at[0], ent)
    l_ret = load(ret_hbm.at[0], ret)

    barrier = pltpu.get_barrier_semaphore()
    near = (0, 1, -1, 2, -2)

    def greet(peers):
        for peer in peers:
            pl.semaphore_signal(barrier, inc=1, device_id=peer, device_id_type=MESH)

    greet([chip(offset) for offset in near[1:]] + [sibling])

    @pl.when(has_previous)
    def _():
        greet([previous(0)])

    @pl.when(has_following)
    def _():
        greet([following(0)])

    l_gain.wait()
    gain = gain_row[...].astype(F32)
    gn[0, 0:1, mine] = gain
    expected = len(near) + jnp.where(has_following, 1, 0) + jnp.where(has_previous, 1, 0)
    pl.semaphore_wait(barrier, expected)

    class Gather:
        groups = {0: (0,), 6: (6, 2), 2: (6, 2), 7: (7, 1), 1: (7, 1), 5: (5, 3, 4), 3: (5, 3, 4), 4: (5, 3, 4)}

        def __init__(self, ref, rows, split, lead=None, deep=False):
            self.ref, self.rows, self.split, self.lead, self.deep = ref, slice(0, rows), split, lead, deep
            self.near, self.far, self.lead_in = {}, {}, {}
            self.far4 = Arrival(ref.at[4, self.rows, mine])
            self.shared, self.lead_shared = {}, {}
            for group in ((0,), (6, 2), (7, 1), (5, 3, 4)):
                span = slice(3, 6) if len(group) == 3 else slice(0, len(group))
                arrival = Arrival(ref.at[span, self.rows, mine])
                self.shared.update({slot: arrival for slot in group})

        def block(self, slot, rows=None):
            return self.ref.at[slot, self.rows if rows is None else rows, mine]

        def lead_row(self, slot):
            return self.lead.at[slot, 0:1, mine]

        def begin(self, offsets=(2, -2, 1, -1)):
            for offset in offsets:
                slot = (-offset) % CHIPS
                if self.lead is not None:
                    self.lead_in[slot] = send(self.lead_row(0), self.lead_row(slot), chip(offset), kind=None)
                self.near[slot] = send(self.block(0), self.block(slot), chip(offset))
                if offset == 2:
                    self.share(0)

        def begin_next(self, src, first):
            for offset in (0, 1, -1) if self.deep else (2, -2, 0, 1, -1):
                slot = (-offset) % CHIPS
                arrival = send(src, self.block(slot), following(offset), kind=2)
                if offset == 0:
                    self.own = arrival
                else:
                    self.near[slot] = arrival
                    send(first, self.block(slot), chip(offset), arrival, kind=3)

        def share_own(self, first):
            @pl.when(has_previous)
            def _():
                self.own.wait()

            @pl.when(no_previous)
            def _():
                self.ref[0, self.rows, mine] = first[...]

            self.share(0)

        def share(self, slot):
            if self.lead is not None:
                self.lead_shared[slot] = send(self.lead_row(slot), self.lead_row(slot), sibling, kind=None)
            send(self.block(slot), self.block(slot), sibling, self.shared[slot])

        def pass_on(self):
            if self.deep:
                for held, step in ((7, 1), (1, -1)):
                    slot = (held - step) % CHIPS
                    if self.lead is not None:
                        self.lead_in[held].wait()
                        self.lead_in[slot] = send(self.lead_row(held), self.lead_row(slot), chip(step), kind=None)
                    self.near[held].wait()
                    self.near[slot] = send(self.block(held), self.block(slot), chip(step))
                    self.share(held)
            else:
                self.pass_far()

        def pass_two(self):
            if self.deep:
                self.pass_far()

        def pass_far(self):
            for held, step in ((6, 1), (2, -1)):
                slot = (held - step) % CHIPS
                if self.lead is not None:
                    self.lead_in[held].wait()
                    self.lead_in[slot] = send(self.lead_row(held), self.lead_row(slot), chip(step), kind=None)
                    if step == 1:
                        self.lead_in[4] = send(self.lead_row(held), self.lead_row(4), chip(2), kind=None)
                self.near[held].wait()
                self.far[slot] = send(self.block(held), self.block(slot), chip(step))
                part = slice(0, self.split) if step == 1 else slice(self.split, self.rows.stop)
                send(self.block(held, part), self.block(4, part), chip(2 * step), self.far4)
                self.share(held)

        def share_near(self):
            for slot in () if self.deep else (7, 1):
                self.near[slot].wait()
                if self.lead is not None:
                    self.lead_in[slot].wait()
                self.share(slot)

        def share_far(self):
            for slot in (5, 3, 4):
                (self.far4 if slot == 4 else self.far[slot]).wait()
                if self.lead is not None:
                    self.lead_in[slot].wait()
                self.share(slot)

        def ready(self, slot):
            self.shared[slot].wait()
            if self.lead is not None:
                self.lead_shared[slot].wait()

    def base_of(slot):
        return pl.multiple_of(lax.rem(y + slot, CHIPS) * PAIR, PAIR)

    def build(slot, norms):
        base = base_of(slot)
        for part in range(3):
            lanes = slice(part * 256, (part + 1) * 256)
            rows = pl.ds(pl.multiple_of(base + part * 256, 256), 256)
            direction = fz[rows, :].astype(F32) + dot_tn(g0[slot, TOK : TOK + RANK, lanes], aout[...])
            w[rows, :] = direction.astype(BF16)
            norms = norms + jnp.sum((direction * direction).reshape(32, 8, COLS), axis=0)
        return norms

    def chunk(ref, slot, squares, total, with_adapter=False):
        z = ref[slot, 0:TOK, :].astype(F32)
        squares = squares + lane_groups(z * z)
        scaled = (z * gn[slot, 0:1, :]).astype(BF16)
        if with_adapter:
            scaled = jnp.concatenate([scaled, ref[slot, TOK : TOK + RANK, :]], axis=0)
        total = total + dot(scaled, w[pl.ds(base_of(slot), PAIR), :])
        return squares, total

    def rscale_of(squares):
        return lax.rsqrt(jnp.sum(squares, axis=1, keepdims=True) / FEATURES + 1e-05)

    def normalise(ref, out, rscale):
        for slot in range(CHIPS):
            z = ref[slot, 0:TOK, :].astype(F32)
            out[slot] = (z * rscale * gn[slot, 0:1, :]).astype(BF16)

    def slope_of(preact):
        sig = 1.0 / (1.0 + jnp.exp(-preact))
        return sig * (1.0 + preact * (1.0 - sig))

    class Scatter:
        def __init__(self, rows, split, pb, sb, sv, rv, back):
            self.rows, self.split = rows, split
            self.pb, self.sb, self.sv, self.rv, self.back = pb, sb, sv, rv, back

        def prepare(self, lhs, ref, rscale, dots, extra=None):
            self.args = lhs, ref, rscale, rscale * rscale * dots / FEATURES, extra

        def compute(self, start, stop):
            lhs, ref, rscale, tilt, extra = self.args
            for n in range(start, stop):
                slot = ORDER[n]
                value = dot_nt(lhs, w[pl.ds(base_of(slot), PAIR), :])
                z = ref[slot, 0:TOK, :].astype(F32)
                scaled = value[0:TOK] * rscale
                term = jnp.sum(scaled * z, axis=0, keepdims=True)
                gt[n : n + 1, :] = term if extra is None else gt[n : n + 1, :] + term
                result = scaled * gn[slot, 0:1, :] - z * tilt
                if extra is not None:
                    result = jnp.concatenate([result, value[TOK:] + extra(slot)], axis=0)
                self.pb[n] = result.astype(BF16)
            return send(self.pb.at[start:stop, :, other], self.sb.at[start:stop], sibling)

        def part(self, start, stop):
            arrival = self.compute(start, stop)
            for n in range(start, stop):
                self.halves[n] = arrival

        def compute_first(self):
            self.halves = {}
            for n in (2, 0, 1):
                self.part(n, n + 1)
            self.part(3, 5)
            self.stage_one()

        def compute_second(self):
            self.part(5, 8)
            self.stage_one_direct()

        def pair_sum(self, n):
            return self.pb[n, :, mine].astype(F32) + self.sb[n].astype(F32)

        def deliver(self, n, offset):
            src, dst = self.sv.at[n], self.rv.at[n]
            if self.back:
                send(src, dst, previous(offset), self.last, kind=1)
            else:
                send(src, dst, chip(offset), self.last)

        def stage_one(self):
            rv, sv = self.rv, self.sv
            self.halves[2].wait()
            sv[2] = self.pair_sum(2).astype(BF16)
            low, high = slice(0, self.split), slice(self.split, self.rows)
            self.r4a = send(sv.at[2, low], rv.at[2, low], chip(-2))
            self.r4b = send(sv.at[2, high], rv.at[2, high], chip(2))
            self.halves[0].wait()
            sv[0] = self.pair_sum(0).astype(BF16)
            self.r1 = send(sv.at[0], rv.at[0], chip(1))
            self.halves[1].wait()
            sv[1] = self.pair_sum(1).astype(BF16)
            self.r2 = send(sv.at[1], rv.at[1], chip(-1))

        def stage_one_direct(self):
            self.halves[3].wait()
            self.last = Arrival(self.rv.at[3:8] if self.back else self.rv.at[3:7])
            for n, offset in ((3, 1), (4, -1)):
                self.sv[n] = self.pair_sum(n).astype(BF16)
                self.deliver(n, offset)

        def stage_two(self):
            rv, split = self.rv, self.split
            self.halves[5].wait()
            if self.back:
                self.sv[7] = self.pair_sum(7).astype(BF16)
                self.deliver(7, 0)
            self.r1.wait()
            self.r4b.wait()
            total = self.pair_sum(5) + rv[0].astype(F32)
            total = jnp.concatenate([total[0:split], total[split:] + rv[2, split:].astype(F32)], axis=0)
            self.sv[5] = total.astype(BF16)
            self.deliver(5, 2)
            self.r2.wait()
            self.r4a.wait()
            total = self.pair_sum(6) + rv[1].astype(F32)
            total = jnp.concatenate([total[0:split] + rv[2, 0:split].astype(F32), total[split:]], axis=0)
            self.sv[6] = total.astype(BF16)
            self.deliver(6, -2)

        def final(self):
            self.last.wait()
            total = self.rv[7].astype(F32) if self.back else self.pair_sum(7)
            for n in (3, 4, 5, 6):
                total = total + self.rv[n].astype(F32)
            return total

    class RowScatter:
        def compute(self):
            self.sib = send(gt.at[:, other], gts, sibling, kind=None)

        def row(self, n, offset):
            return send(gtv.at[n : n + 1], gtr.at[n : n + 1], chip(offset), kind=None)

        def stage_one(self):
            self.sib.wait()
            gtv[...] = gt[:, mine] + gts[...]
            self.inner = [self.row(0, 1), self.row(1, -1), self.row(2, -2)]
            self.last = [self.row(3, 1), self.row(4, -1)]

        def stage_two(self):
            for copy in self.inner:
                copy.wait()
            gtv[5:6] = gtv[5:6] + gtr[0:1]
            gtv[6:7] = gtv[6:7] + gtr[1:2] + gtr[2:3]
            self.last += [self.row(5, 2), self.row(6, -2)]

        def final(self):
            for copy in self.last:
                copy.wait()
            return gtv[7:8] + gtr[3:4] + gtr[4:5] + gtr[5:6] + gtr[6:7]

    ga_s0 = Gather(g0, TOK + RANK, 48, lead=gn)
    ga_t0 = Gather(g1, TOK, 32)
    ga_s1 = Gather(g2, TOK, 32)
    ga_t1 = Gather(g3, TOK, 32)
    rs0 = Scatter(TOK, 32, pb0, sb0, sv0, rv0, True)
    rs1 = Scatter(TOK + RANK, 48, pb1, sb1, sv1, rv1, False)
    rows = RowScatter()

    def fresh():
        return jnp.zeros((TOK, 128), F32), jnp.zeros((TOK, COLS), F32)

    l_s0.wait()
    l_a.wait()
    ga_s0.begin()
    l_tg.wait()
    early_cot = send(tg, tgx, previous(0), kind=1)
    l_fz.wait()
    l_p.wait()
    norms = jnp.zeros((8, COLS), F32)
    squares = jnp.zeros((TOK, 128), F32)
    total = jnp.zeros((TOK + RANK, COLS), F32)
    ga_s0.ready(0)
    norms = build(0, norms)
    squares, total = chunk(g0, 0, squares, total, True)
    ga_s0.pass_on()
    ga_s0.pass_two()
    l_t0.wait()
    ga_t0.begin()
    ga_s0.share_near()
    for slot in (6, 2, 7, 1):
        ga_s0.ready(slot)
        norms = build(slot, norms)
        squares, total = chunk(g0, slot, squares, total, True)
    ga_s0.share_far()
    ga_t0.pass_on()
    ga_t0.pass_two()
    l_s1.wait()
    ga_s1.begin()
    for slot in (5, 3, 4):
        ga_s0.ready(slot)
        norms = build(slot, norms)
        squares, total = chunk(g0, slot, squares, total, True)
    norm_squares = jnp.sum(norms, axis=0, keepdims=True) + 1e-06
    colnorm = jnp.sqrt(norm_squares)
    l_mag.wait()
    col_scale = mag[...] / colnorm
    r0 = rscale_of(squares)
    raw0 = total[0:TOK] * r0
    adapter_direction = total[TOK:]
    preact = raw0 * col_scale
    pg = tg[...].astype(F32) * slope_of(preact)
    pgs0 = (pg * col_scale).astype(BF16)
    inner = jnp.sum(pg * raw0, axis=0, keepdims=True)
    rs0.prepare(pgs0, g0, r0, jnp.sum(pg * preact, axis=1, keepdims=True))
    rs0.compute_first()
    rs0.compute_second()
    ga_t0.share_near()
    ga_s1.pass_on()
    ga_s1.pass_two()
    ga_t0.share_far()
    squares, total = fresh()
    for slot in (0, 7, 1, 6, 2):
        ga_t0.ready(slot)
        squares, total = chunk(g1, slot, squares, total)
    rs0.stage_two()
    for slot in (5, 3, 4):
        ga_t0.ready(slot)
        squares, total = chunk(g1, slot, squares, total)
    preact = total * rscale_of(squares) * col_scale
    em[...] = (g1[0, :, mine].astype(F32) + preact / (1.0 + jnp.exp(-preact))).astype(BF16)
    l_ent.wait()
    ga_t1.begin_next(em, ent)
    ga_s1.share_near()
    normalise(g0, zn0, r0)
    factor = aout[...]
    weights0 = dot_nt(factor, pgs0)
    ga_s1.share_far()
    squares1, total1 = fresh()
    for slot in (0, 7, 1, 6, 2):
        ga_s1.ready(slot)
        squares1, total1 = chunk(g2, slot, squares1, total1)
    for slot in (5, 3, 4):
        ga_s1.ready(slot)
        squares1, total1 = chunk(g2, slot, squares1, total1)
    r1 = rscale_of(squares1)
    raw1 = total1 * r1
    preact1 = raw1 * col_scale
    slope = slope_of(preact1)
    normalise(g2, zn1, r1)
    ga_t1.share_own(ent)
    ga_t1.pass_on()
    ga_t1.pass_two()
    l_ret.wait()

    @pl.when(has_following)
    def _():
        early_cot.wait()
        gx[...] = (tgx[...].astype(F32) + rs0.final()).astype(BF16)

    @pl.when(jnp.logical_not(has_following))
    def _():
        gx[...] = ret[...]

    cot1 = gx[...].astype(F32)
    pg = cot1 * slope
    pgs1 = (pg * col_scale).astype(BF16)
    inner = inner + jnp.sum(pg * raw1, axis=0, keepdims=True)
    scaled_ratio = col_scale * inner / norm_squares
    weights = jnp.concatenate([weights0, dot_nt(factor, pgs1)], axis=1).astype(BF16)
    shrunk = (factor.astype(F32) * -scaled_ratio).astype(BF16)

    def column_extra(slot):
        return dot(weights, jnp.concatenate([zn0[slot], zn1[slot]], axis=0))

    rs1.prepare(
        jnp.concatenate([pgs1, shrunk], axis=0), g2, r1, jnp.sum(pg * preact1, axis=1, keepdims=True), column_extra
    )
    rs1.compute_first()
    rs1.compute_second()
    rows.compute()
    ga_t1.share_near()
    packed[160:168] = jnp.zeros((8, COLS), F32)
    packed[160:161] = inner / colnorm
    product = jnp.zeros((RANK, TOK * SLOTS), F32)
    for slot in range(CHIPS):
        product = product + dot_nt(
            g0[slot, TOK : TOK + RANK, :], jnp.concatenate([zn0[slot], zn1[slot]], axis=0)
        )
    upper = product.astype(BF16)
    lower = (product - upper.astype(F32)).astype(BF16)
    both = dot(jnp.concatenate([upper, lower], axis=0), jnp.concatenate([pgs0, pgs1], axis=0))
    packed[144:160] = both[0:RANK] + both[RANK:] - adapter_direction * scaled_ratio
    rows.stage_one()
    rs1.stage_two()
    rows.stage_two()
    squares, total = fresh()
    for slot in (0, 7, 1, 6, 2):
        ga_t1.ready(slot)
        squares, total = chunk(g3, slot, squares, total)
    ga_t1.share_far()
    for slot in (5, 3, 4):
        ga_t1.ready(slot)
        squares, total = chunk(g3, slot, squares, total)
    preact = total * rscale_of(squares) * col_scale
    packed[0:64] = g3[0, :, mine].astype(F32) + preact / (1.0 + jnp.exp(-preact))
    packed[161:162] = rows.final()
    result = rs1.final()
    packed[128:144] = result[TOK:]
    packed[64:128] = cot1 + result[0:TOK]
    for copy in alone:
        copy.wait_send()
    for kind, condition in enumerate(conditions):
        everything = w.at[0 : sent[kind]]
        copy = pltpu.make_async_copy(everything, everything, ssem.at[kind])
        if condition is None:
            copy.wait()
        else:
            pl.when(condition)(copy.wait)


def hand_out(packed, act, grad, mag, grad_in, grad_out, gain):
    mean = 1.0 / (SLOTS * TOK)
    act[0] = packed[0:64].astype(BF16)
    grad[0] = packed[64:128].astype(BF16)
    grad_in[0] = packed[128:144] * mean
    grad_out[0] = packed[144:160] * mean
    mag[...] = packed[160:161] * mean
    gain[...] = packed[161:162] * mean


def local(*args):
    hbm = pl.BlockSpec(memory_space=pltpu.HBM)
    vmem = pl.BlockSpec(memory_space=pltpu.VMEM)
    rows1 = TOK + RANK

    def scatter_buffers(rows):
        return [
            pltpu.VMEM((8, rows, PAIR), BF16),
            pltpu.VMEM((8, rows, COLS), BF16),
            pltpu.VMEM((8, rows, COLS), BF16),
            pltpu.VMEM((8, rows, COLS), BF16),
        ]

    gathered = pltpu.VMEM((CHIPS, TOK, PAIR), BF16)
    block = pltpu.VMEM((TOK, COLS), BF16)
    out_shape = (
        jax.ShapeDtypeStruct((1, TOK, COLS), BF16),
        jax.ShapeDtypeStruct((1, TOK, COLS), BF16),
        jax.ShapeDtypeStruct((1, COLS), F32),
        jax.ShapeDtypeStruct((1, RANK, COLS), F32),
        jax.ShapeDtypeStruct((1, RANK, COLS), F32),
        jax.ShapeDtypeStruct((1, COLS), F32),
    )
    packed = pl.pallas_call(
        kernel,
        out_shape=jax.ShapeDtypeStruct((168, COLS), F32),
        in_specs=[hbm] * 10,
        out_specs=vmem,
        scratch_shapes=[
            pltpu.VMEM((1, COLS), F32),
            pltpu.VMEM((1, COLS), BF16),
            pltpu.VMEM((FEATURES, COLS), BF16),
            pltpu.VMEM((FEATURES, COLS), BF16),
            pltpu.VMEM((CHIPS, rows1, PAIR), BF16),
            gathered,
            gathered,
            gathered,
            pltpu.VMEM((CHIPS, 8, PAIR), F32),
            gathered,
            gathered,
            block,
            block,
            block,
            block,
            pltpu.VMEM((RANK, COLS), BF16),
            block,
            block,
            *scatter_buffers(TOK),
            *scatter_buffers(rows1),
            pltpu.VMEM((8, PAIR), F32),
            pltpu.VMEM((8, COLS), F32),
            pltpu.VMEM((8, COLS), F32),
            pltpu.VMEM((8, COLS), F32),
            pltpu.SemaphoreType.DMA((DEPARTURES,)),
            pltpu.SemaphoreType.DMA((ARRIVALS,)),
            pltpu.SemaphoreType.DMA((11,)),
        ],
        compiler_params=pltpu.CompilerParams(
            collective_id=0, has_side_effects=True, vmem_limit_bytes=56 * 2**20
        ),
        name="window",
    )(*args)
    return pl.pallas_call(
        hand_out, out_shape=out_shape, in_specs=[vmem], out_specs=(vmem,) * 6, name="hand_out"
    )(packed)


def solution(mesh):
    in_specs = (
        P("section", None, "tensor"),
        P(None, None, "tensor"),
        P("section", None, None, "tensor"),
        P("section", None, "tensor"),
        P(None, None, "tensor"),
        P("section", None, "tensor"),
        P("section", None, "tensor"),
        P("section", None, "tensor"),
        P("section", "tensor"),
        P("section", "tensor"),
    )
    out_specs = (
        P("section", None, "tensor"),
        P("section", None, "tensor"),
        P("section", "tensor"),
        P("section", None, "tensor"),
        P("section", None, "tensor"),
        P("section", "tensor"),
    )
    return jax.shard_map(local, mesh=mesh, in_specs=in_specs, out_specs=out_specs, check_vma=False)
```
